256 devices in a mesh: dp: 4 (over y), seq: 8 (over x, core), tensor: 8 (over z).
Axes of the slice: x: 4, y: 4, z: 8, core: 2. Of those that a mesh axis runs over, the one named last changes fastest.
Arguments:
- x_in: bfloat16 [4, 4096, 8192], P('dp', 'seq', 'tensor'), may hold values from -0.0625 to 0.0625
- b_in: bfloat16 [4, 4096, 1024], P('dp', 'seq', 'tensor'), may hold values from -3 to 3
- c_in: bfloat16 [4, 4096, 1024], P('dp', 'seq', 'tensor'), may hold values from -3 to 3
- log_decay: float32 [4, 4096, 128], P('dp', 'seq', 'tensor'), may hold values from -1 to 0, as said below
- out_weight: bfloat16 [8192, 4096], P('tensor'), may hold values from -0.0625 to 0.0625
- out_grad: bfloat16 [4, 4096, 4096], P('dp', 'seq', 'tensor'), may hold values from -0.078125 to 0.078125
Outputs:
- weight_grad: bfloat16 [8192, 4096], P('tensor', ('dp', 'seq'))
- x_grad: bfloat16 [4, 4096, 8192], P('dp', 'seq', 'tensor')
- b_grad: bfloat16 [4, 4096, 1024], P('dp', 'seq', 'tensor')
- c_grad: bfloat16 [4, 4096, 1024], P('dp', 'seq', 'tensor')
The draws below stay inside these ranges and needn't reach their ends.
Inputs may be any that keep to these rules, and one draw needn't show every extreme that they name: `log_decay`: every log-decay is below zero.
All inputs are finite; a program needn't handle non-finite values.
Results may differ from the reference program's by a relative error of at most 0.017.
Values may be sent and summed in bfloat16 or wider, within the bound.
A program may use at most 192 MiB of HBM per device.

```python
import math
import jax
import jax.numpy as jnp
from jax import lax

WIDTH = 4096
HEADS = 128
HEAD_DIM = 64
STATE = 128
GROUPS = 8
SPAN = 256
INNER = 8192
REPO_COUNT = 4
REPO_TOKENS = 4096


def draw_log_decay(key, part):
    split_keys = jax.random.split(key, 7)
    keep_tenths = 5
    is_slow = jax.random.randint(split_keys[0], (HEADS,), 0, 10) < keep_tenths
    slow_rate = math.log(10.0) / REPO_TOKENS * jax.random.uniform(split_keys[1], (HEADS,), minval=0.1, maxval=0.4)
    fast_rate = jnp.exp(jax.random.uniform(split_keys[2], (HEADS,), minval=math.log(1.0 / 50.0), maxval=math.log(1.0 / 20.0)))
    decay_factors = jnp.where(is_slow, slow_rate, fast_rate)
    block_list = jnp.exp(jax.random.uniform(split_keys[3], (REPO_COUNT, REPO_TOKENS // SPAN, HEADS), minval=math.log(0.5), maxval=math.log(2.0)))
    block_list = jnp.repeat(block_list, SPAN, axis=1)
    jitter_level = jax.random.uniform(split_keys[4], (REPO_COUNT, REPO_TOKENS, HEADS), minval=0.3, maxval=1.7)
    spike_positions = jax.random.randint(split_keys[5], (REPO_COUNT, 2), 0, REPO_TOKENS)
    loss_values = jax.random.uniform(split_keys[6], (REPO_COUNT, 2, HEADS), minval=0.2, maxval=0.4)
    at_position = (jnp.arange(REPO_TOKENS)[None, :, None] == spike_positions[:, None, :]).astype(jnp.float32)
    spike_values = jnp.sum(at_position[..., None] * (-jnp.log(1.0 - loss_values))[:, None], axis=2)
    return -(decay_factors * block_list * jitter_level + spike_values)


def strengthened(drawn, stream_key, source, target, shards_of, factor):
    def block_of(axis_at):
        return (jnp.arange(drawn.shape[axis_at]) // (drawn.shape[axis_at] // shards_of)).reshape((-1,) + (1,) * (drawn.ndim - 1 - axis_at))

    first = jax.random.permutation(stream_key, shards_of)[block_of(target)]
    other_side = (block_of(target) + shards_of // 2) % shards_of
    return jnp.where((block_of(source) == first) | (block_of(source) == other_side), factor * drawn, drawn)


def shard_levels(own_key, extent, cuts, smallest, largest):
    loudness = 1.0
    for axis_at, shards_of in cuts:
        heights = jax.random.uniform(jax.random.fold_in(jax.random.fold_in(own_key, 6), axis_at), (shards_of,), jnp.float32, smallest / len(cuts), largest / len(cuts))
        loudness = loudness * jnp.repeat(jnp.exp(heights), extent[axis_at] // shards_of).reshape((-1,) + (1,) * (len(extent) - 1 - axis_at))
    return loudness


def normal_values(key, dims, scale, limit, cuts=(), dtype=jnp.bfloat16):
    array = scale * jax.random.normal(key, dims, jnp.float32)
    if cuts:
        array = array * shard_levels(key, dims, cuts, -0.22, 0.18)
    return jnp.clip(array, -limit, limit).astype(dtype)


def noise_with(own_key, dims, scale, reach, cuts, heavy, kind=jnp.bfloat16):
    values = scale * jax.random.normal(own_key, dims, jnp.float32)
    if cuts:
        values = values * shard_levels(own_key, dims, cuts, -0.22, 0.18)
    return jnp.clip(strengthened(values, jax.random.fold_in(own_key, 3), *heavy), -reach, reach).astype(kind)


def setup_inputs(seed: int = 0) -> dict:
    keys = jax.random.split(jax.random.key(seed), 7)
    x_in = normal_values(keys[0], (REPO_COUNT, REPO_TOKENS, INNER), 0.01, 0.0625, ((0, 4), (1, 8), (2, 8)))
    b_in = normal_values(keys[1], (REPO_COUNT, REPO_TOKENS, GROUPS * STATE), 0.5, 3.0, ((0, 4), (1, 8), (2, 8)))
    c_in = normal_values(keys[2], (REPO_COUNT, REPO_TOKENS, GROUPS * STATE), 0.5, 3.0, ((0, 4), (1, 8), (2, 8)))
    log_decay = draw_log_decay(jax.random.fold_in(keys[6], 71), 0)
    out_weight = normal_values(keys[4], (INNER, WIDTH), INNER ** -0.5, 0.0625, ((0, 8),))
    out_grad = noise_with(keys[5], (REPO_COUNT, REPO_TOKENS, WIDTH), 0.01, 0.078125, ((0, 4), (1, 8), (2, 8)), (1, 2, 8, 2.0))
    return dict(x_in=x_in, b_in=b_in, c_in=c_in, log_decay=log_decay, out_weight=out_weight, out_grad=out_grad)


highest = lax.Precision.HIGHEST

def decay_terms(decays):
    running = jnp.cumsum(decays, axis=1)
    totals = running[:, -1]
    by_head = jnp.transpose(running, (0, 2, 3, 1))
    spread = by_head[..., :, None] - by_head[..., None, :]
    places = jnp.arange(decays.shape[1])
    causal = places[:, None] >= places[None, :]
    within = jnp.where(causal, jnp.exp(jnp.minimum(spread, 0.0)), 0.0)
    to_end = jnp.exp(totals[:, None] - running)
    from_start = jnp.exp(running)
    return (totals, within, to_end, from_start)

def forward_states(totals, span_adds):

    def advance(carried, inputs):
        return (jnp.exp(inputs[0])[..., None, None] * carried + inputs[1], carried)
    last_state, entering = lax.scan(advance, jnp.zeros_like(span_adds[0]), (totals, span_adds))
    return (entering, last_state)

def item_forward(values, writes, read_rows, decays):
    totals, within, to_end, from_start = decay_terms(decays)
    affinity = jnp.einsum('cign,cjgn->cgij', read_rows, writes, precision=highest)
    weights = affinity[:, :, None] * within
    inner_out = jnp.einsum('cgrij,cjgrp->cigrp', weights, values, precision=highest)
    span_adds = jnp.einsum('cjgn,cjgrp->cgrnp', writes, to_end[..., None] * values, precision=highest)
    entering, last_state = forward_states(totals, span_adds)
    carried_out = jnp.einsum('cign,cgrnp->cigrp', read_rows, entering, precision=highest)
    return inner_out + carried_out * from_start[..., None]

def reference(x_in, b_in, c_in, log_decay, out_weight, out_grad):
    per_group = HEADS // GROUPS
    spans = REPO_TOKENS // SPAN
    item_count = REPO_COUNT * GROUPS
    y_grad = jnp.dot(out_grad.reshape(REPO_COUNT * REPO_TOKENS, WIDTH), out_weight.T, preferred_element_type=jnp.float32).astype(jnp.bfloat16)

    def heads_first(source):
        shaped = source.astype(jnp.float32).reshape(REPO_COUNT, REPO_TOKENS, GROUPS, per_group, HEAD_DIM)
        return shaped.transpose(0, 2, 1, 3, 4).reshape(item_count, spans, SPAN, 1, per_group, HEAD_DIM)

    def groups_first(source):
        shaped = source.astype(jnp.float32).reshape(REPO_COUNT, REPO_TOKENS, GROUPS, STATE)
        return shaped.transpose(0, 2, 1, 3).reshape(item_count, spans, SPAN, 1, STATE)
    decays = log_decay.reshape(REPO_COUNT, REPO_TOKENS, GROUPS, per_group).transpose(0, 2, 1, 3)
    decays = decays.reshape(item_count, spans, SPAN, 1, per_group)

    def per_item(inputs):
        values, writes, read_rows, decay_item, grad_item = inputs
        outputs, pullback = jax.vjp(lambda value_arg, write_arg, read_arg: item_forward(value_arg, write_arg, read_arg, decay_item), values, writes, read_rows)
        gradients = pullback(grad_item)
        return (outputs, gradients[0], gradients[1], gradients[2])
    scan_out, x_part, b_part, c_part = lax.map(per_item, (heads_first(x_in), groups_first(b_in), groups_first(c_in), decays, heads_first(y_grad.reshape(REPO_COUNT, REPO_TOKENS, INNER))))

    def heads_back(source):
        return source.reshape(REPO_COUNT, GROUPS, REPO_TOKENS, per_group * HEAD_DIM).transpose(0, 2, 1, 3).reshape(REPO_COUNT, REPO_TOKENS, INNER)

    def groups_back(source):
        return source.reshape(REPO_COUNT, GROUPS, REPO_TOKENS, STATE).transpose(0, 2, 1, 3).reshape(REPO_COUNT, REPO_TOKENS, GROUPS * STATE)
    scan_rows = heads_back(scan_out).astype(jnp.bfloat16)
    weight_grad = jnp.dot(scan_rows.reshape(REPO_COUNT * REPO_TOKENS, INNER).T, out_grad.reshape(REPO_COUNT * REPO_TOKENS, WIDTH), preferred_element_type=jnp.float32).astype(jnp.bfloat16)
    return (weight_grad, heads_back(x_part).astype(jnp.bfloat16), groups_back(b_part).astype(jnp.bfloat16), groups_back(c_part).astype(jnp.bfloat16))
```

```python
from types import SimpleNamespace

import jax
import jax.numpy as jnp
from jax import lax
from jax.experimental import pallas as pl
from jax.experimental.pallas import tpu as pltpu
from jax.sharding import PartitionSpec as P

F32 = jnp.float32
BF16 = jnp.bfloat16
MESH = pl.DeviceIdType.MESH
NEG = -1e30

VMEM_SCRATCH = dict(
    xv=((512, 1024), BF16),
    bv=((512, 128), BF16),
    cv=((512, 128), BF16),
    dv=((512, 16), F32),
    wv=((8, 1024, 512), BF16),
    cot=((8, 512, 512), BF16),
    cot_sib=((8, 512, 256), BF16),
    b_t=((2, 128, 256), BF16),
    c_t=((2, 128, 256), BF16),
    la=((16, 512, 128), F32),
    la_row=((32, 8, 256), F32),
    tots=((2, 2, 8, 512), F32),
    aff=((2, 256, 256), F32),
    aff_t=((2, 256, 256), F32),
    within_t=((32, 3, 128, 128), BF16),
    weights_t=((32, 3, 128, 128), BF16),
    x_end=((512, 1024), BF16),
    inner=((512, 1024), F32),
    y_acc=((512, 1024), F32),
    gy=((512, 1024), BF16),
    gy_start=((512, 1024), BF16),
    scan_t=((1024, 512), BF16),
    scan_t_sib=((1024, 512), BF16),
    adds=((2, 2, 128, 512), F32),
    loc=((2, 2, 128, 512), F32),
    inc=((2, 2, 128, 512), F32),
    inh=((128, 512), F32),
    ent=((2, 2, 128, 512), BF16),
    lv=((2, 2, 128, 512), BF16),
    l1_out=((2, 2, 128, 512), BF16),
    l1_in=((2, 128, 512), BF16),
    l2_out=((2, 128, 512), BF16),
    l2_in=((2, 3, 128, 512), BF16),
    l3_out=((2, 128, 512), BF16),
    l3_in=((2, 128, 512), BF16),
    d_own=((2, 8, 512), F32),
    d_sib=((8, 512), F32),
    d_chip=((4, 8, 512), F32),
    part=((8, 1024, 256), BF16),
    xa_in=((4, 3, 512, 128), BF16),
    ya_in=((2, 3, 512, 256), BF16),
    xq=((4, 512, 128), BF16),
    yq=((2, 512, 256), BF16),
    xb_in=((3, 512, 128), BF16),
    yb_in=((3, 512, 128), BF16),
    aff_grad=((2, 256, 256), F32),
    x_out=((512, 1024), BF16),
    b_out=((512, 128), BF16),
    c_out=((512, 128), BF16),
    w_out=((1024, 128), BF16),
)
SEMAPHORES = dict(
    load=(6,),
    load_w=(8,),
    right_s=(7,),
    right_r=(7,),
    left_s=(7,),
    left_r=(7,),
    sib_s=(32,),
    sib_r=(32,),
    scan_s=(1,),
    scan_r=(1,),
    ds_s=(1,),
    ds_r=(1,),
    dc_s=(4,),
    dc_r=(4,),
    l1_s=(2,),
    l1_r=(2,),
    l2_s=(6,),
    l2_r=(6,),
    l3_s=(2,),
    l3_r=(2,),
    xa_s=(16,),
    xa_r=(12,),
    ya_s=(8,),
    ya_r=(6,),
    xb_s=(4,),
    xb_r=(3,),
    yb_s=(4,),
    yb_r=(3,),
    store=(4,),
)
NAMES = list(VMEM_SCRATCH) + [f"{n}_sem" for n in SEMAPHORES]


def mm(a, b):
    return jnp.dot(a, b, preferred_element_type=F32)


def mm_nt(a, b):
    return lax.dot_general(a, b, (((1,), (1,)), ((), ())), preferred_element_type=F32)


def at128(i, size=128):
    return pl.ds(pl.multiple_of(i * 128, 128), size)


def at256(i, size=256):
    return pl.ds(pl.multiple_of(i * 256, 256), size)


def split3(v):
    hi = v.astype(BF16)
    rest = v - hi.astype(F32)
    mid = rest.astype(BF16)
    return hi, mid, (rest - mid.astype(F32)).astype(BF16)


def kernel(x_hbm, b_hbm, c_hbm, d_hbm, w_hbm, g_hbm, wg_hbm, xg_hbm, bg_hbm, cg_hbm, *scratch):
    S = SimpleNamespace(**dict(zip(NAMES, scratch)))
    y = lax.axis_index("dp")
    s = lax.axis_index("seq")
    z = lax.axis_index("tensor")
    x = s // 2
    c = s % 2
    sib = (y, x * 2 + (1 - c), z)
    right = (y, s, (z + 1) % 8)
    left = (y, s, (z + 7) % 8)

    def x_peer(xx):
        return (y, xx * 2 + c, z)

    def y_peer(yy):
        return (yy, s, z)

    def remote(src, dst, send_sem, recv_sem, device):
        return pltpu.make_async_remote_copy(
            src_ref=src,
            dst_ref=dst,
            send_sem=send_sem,
            recv_sem=recv_sem,
            device_id=device,
            device_id_type=MESH,
        )

    loads = [
        pltpu.make_async_copy(d_hbm.at[0], S.dv, S.load_sem.at[0]),
        pltpu.make_async_copy(b_hbm.at[0], S.bv, S.load_sem.at[1]),
        pltpu.make_async_copy(c_hbm.at[0], S.cv, S.load_sem.at[2]),
        pltpu.make_async_copy(x_hbm.at[0], S.xv, S.load_sem.at[3]),
        pltpu.make_async_copy(g_hbm.at[0], S.cot.at[z], S.load_sem.at[4]),
    ]
    for load in loads:
        load.start()

    def load_w(k):
        return pltpu.make_async_copy(
            w_hbm.at[:, pl.ds(pl.multiple_of(k * 512, 512), 512)], S.wv.at[k], S.load_w_sem.at[k]
        )

    load_w(z).start()

    barrier = pltpu.get_barrier_semaphore()
    peers = [sib, right, left]
    peers += [x_peer((x + i) % 4) for i in (1, 2, 3)] + [y_peer((y + i) % 4) for i in (1, 2, 3)]
    for peer in peers:
        pl.semaphore_signal(barrier, inc=1, device_id=peer, device_id_type=MESH)
    pl.semaphore_wait(barrier, len(peers))

    def ring(u, k_right, k_left, own=False):
        half_r = u % 2
        half_l = 1 - u % 2
        rows_r = at256(half_r)
        rows_l = at256(half_l)
        src_r = g_hbm.at[0, rows_r] if own else S.cot.at[k_right, rows_r]
        src_l = g_hbm.at[0, rows_l] if own else S.cot.at[k_left, rows_l]
        return (
            remote(src_r, S.cot.at[k_right, rows_r], S.right_s_sem.at[u], S.right_r_sem.at[u], right),
            remote(src_l, S.cot.at[k_left, rows_l], S.left_s_sem.at[u], S.left_r_sem.at[u], left),
        )

    for u in (0, 1):
        for copy in ring(u, z, z, own=True):
            copy.start()

    def start_w(i, carry):
        load_w((z + i) % 8).start()
        return carry

    lax.fori_loop(1, 8, start_w, 0)

    def sib_columns(k, half):
        copies = []
        for j in (0, 1):
            i = k * 4 + half * 2 + j
            copies.append(
                remote(
                    S.cot.at[k, at256(half), at128(2 * j + 1 - c)],
                    S.cot_sib.at[k, at256(half), pl.ds(j * 128, 128)],
                    S.sib_s_sem.at[i],
                    S.sib_r_sem.at[i],
                    sib,
                )
            )
        return copies

    def y_block(k, half, first=False):
        rows = at256(half)

        def tile(n, carry):
            cols = at256(n)
            part = mm_nt(S.cot[k, rows, :], S.wv[k, cols, :])
            if first:
                S.y_acc[rows, cols] = part
            else:
                S.y_acc[rows, cols] += part
            return carry

        lax.fori_loop(0, 4, tile, 0)

    def ring_step(t):
        d = t // 2 + 1
        k_right = (z + 8 - d) % 8
        k_left = (z + d) % 8
        for copy in ring(t, k_right, k_left):
            copy.wait_recv()

        @pl.when(t <= 4)
        def _():
            for copy in ring(t + 2, k_right, k_left):
                copy.start()

        for copy in sib_columns(k_right, t % 2) + sib_columns(k_left, 1 - t % 2):
            copy.start()
        y_block(k_right, t % 2)
        y_block(k_left, 1 - t % 2)

    def iota(shape, dim):
        return lax.broadcasted_iota(jnp.int32, shape, dim)

    low_lanes = iota((256, 128), 1) < 64
    lane_row = iota((1, 128), 1)
    lane_masks = [
        jnp.where(lane_row < 64, 1.0, 0.0).astype(BF16),
        jnp.where(lane_row < 64, 0.0, 1.0).astype(BF16),
    ]
    lower = iota((128, 128), 0) >= iota((128, 128), 1)
    upper = iota((128, 128), 1) >= iota((128, 128), 0)

    loads[0].wait()
    place = jnp.where(iota((16, 128), 0) == iota((16, 128), 1), 1.0, 0.0).astype(BF16)
    tril = jnp.where(iota((256, 256), 0) >= iota((256, 256), 1), 1.0, 0.0).astype(BF16)
    for sp in (0, 1):
        rows = pl.ds(sp * 256, 256)
        padded = sum(mm(p, place) for p in split3(S.dv[rows, :]))
        running = sum(mm(tril, p) for p in split3(padded))
        for h in range(16):
            S.la[h, rows, :] = jnp.broadcast_to(running[:, h : h + 1], (256, 128))
        turned = running.T
        for h in range(16):
            S.la_row[sp * 16 + h] = jnp.broadcast_to(turned[h : h + 1, :], (8, 256))

    def pair_log(rows, hp):
        return jnp.where(low_lanes, S.la[2 * hp, rows, :], S.la[2 * hp + 1, rows, :])

    def where_of(it):
        sp = it // 8
        hp = it % 8
        return sp, hp, at256(sp), at128(hp), hp // 4, at128(hp % 4)

    for load in loads[1:4]:
        load.wait()
    for sp in (0, 1):
        rows = pl.ds(sp * 256, 256)
        S.b_t[sp] = S.bv[rows, :].astype(F32).T.astype(BF16)
        S.c_t[sp] = S.cv[rows, :].astype(F32).T.astype(BF16)

    def span_add(it, carry):
        sp, hp, rows, lanes, half, half_lanes = where_of(it)
        logs = pair_log(rows, hp)
        total = logs[255:256, :]
        S.tots[sp, half, :, half_lanes] = jnp.broadcast_to(total, (8, 128))
        scaled = (jnp.exp(total - logs) * S.xv[rows, lanes].astype(F32)).astype(BF16)
        S.x_end[rows, lanes] = scaled
        S.adds[sp, half, :, half_lanes] = mm(S.b_t[sp], scaled)
        return carry

    lax.fori_loop(0, 16, span_add, 0)

    def row(ref):
        return ref[0:1, :]

    def exchange_1(way):
        for half in (0, 1):
            S.l1_out[way, half] = S.loc[way, half].astype(BF16)
        l1_copy(way).start()

    def l1_copy(way):
        return remote(
            S.l1_out.at[way, 1 - c], S.l1_in.at[way], S.l1_s_sem.at[way], S.l1_r_sem.at[way], sib
        )

    def l2_copy(way, dist):
        to = x + dist if way == 0 else x - dist
        i = way * 3 + dist - 1
        return remote(
            S.l2_out.at[way],
            S.l2_in.at[way, dist - 1],
            S.l2_s_sem.at[i],
            S.l2_r_sem.at[i],
            x_peer(to),
        )

    def l3_copy(way):
        return remote(S.l3_out.at[way], S.l3_in.at[way], S.l3_s_sem.at[way], S.l3_r_sem.at[way], sib)

    def place_of(way):
        return (c, x) if way == 0 else (1 - c, 3 - x)

    def exchange_2(way):
        core, chip = place_of(way)
        l1_copy(way).wait_recv()
        one = jnp.ones((1, 512), F32)
        a = jnp.where(core == 0, jnp.exp(row(S.d_sib)), one)
        b = jnp.where(core == 0, one, jnp.exp(S.d_own[c, 0:1, :]))
        S.l2_out[way] = (a * S.loc[way, c] + b * S.l1_in[way].astype(F32)).astype(BF16)
        for dist in (1, 2, 3):

            @pl.when(chip + dist <= 3)
            def _():
                l2_copy(way, dist).start()

    def exchange_3(way):
        core, chip = place_of(way)
        S.inh[...] = jnp.zeros_like(S.inh)
        near = 3 if way == 0 else 1
        for dist in (1, 2, 3):

            @pl.when(chip >= dist)
            def _():
                l2_copy(way, dist).wait_recv()
                term = S.l2_in[way, dist - 1].astype(F32)
                if dist == 2:
                    term = term * jnp.exp(S.d_chip[near, 0:1, :])
                if dist == 3:
                    term = term * jnp.exp(S.d_chip[near, 0:1, :] + S.d_chip[2, 0:1, :])
                S.inh[...] += term

        into = S.inh[...]
        own = S.loc[way, c] + jnp.exp(S.d_own[c, 0:1, :]) * into
        S.l3_out[way] = jnp.where(core == 0, own, into).astype(BF16)
        l3_copy(way).start()
        other = S.l1_in[way].astype(F32) + jnp.exp(row(S.d_sib)) * into
        S.inc[way, c] = jnp.where(core == 0, into, other)

    def exchange_4(way):
        l3_copy(way).wait_recv()
        S.inc[way, 1 - c] = S.l3_in[way].astype(F32)

    def d_sib_copy():
        return remote(S.d_own.at[1 - c], S.d_sib, S.ds_s_sem.at[0], S.ds_r_sem.at[0], sib)

    def d_chip_copy(dist):
        return remote(
            S.d_chip.at[0],
            S.d_chip.at[4 - dist],
            S.dc_s_sem.at[dist],
            S.dc_r_sem.at[4 - dist],
            x_peer((x + dist) % 4),
        )

    for half in (0, 1):
        S.d_own[half] = S.tots[0, half] + S.tots[1, half]
        S.loc[0, half] = jnp.exp(S.tots[1, half, 0:1, :]) * S.adds[0, half] + S.adds[1, half]
    d_sib_copy().start()
    exchange_1(0)

    loads[4].wait()
    for half in (0, 1):
        for copy in sib_columns(z, half):
            copy.start()
    load_w(z).wait()
    for half in (0, 1):
        y_block(z, half, first=True)

    d_sib_copy().wait_recv()
    S.d_chip[0] = S.d_own[c] + S.d_sib[...]
    for dist in (1, 2, 3):
        d_chip_copy(dist).start()
    exchange_2(0)

    for sp in (0, 1):
        rows = pl.ds(sp * 256, 256)
        S.aff[sp] = mm_nt(S.cv[rows, :], S.bv[rows, :])
        S.aff_t[sp] = mm_nt(S.bv[rows, :], S.cv[rows, :])

    def within_span(it, carry):
        sp, hp, rows, lanes, half, half_lanes = where_of(it)
        values = S.xv[rows, lanes]
        top = jnp.zeros((128, 128), F32)
        bottom = jnp.zeros((128, 128), F32)
        for u in (0, 1):
            col = S.la[2 * hp + u, rows, :]
            line = S.la_row[sp * 16 + 2 * hp + u, 0:1, :]
            tl = jnp.exp(jnp.where(lower, col[:128] - line[:, :128], NEG)) * S.aff[sp, :128, :128]
            bl = jnp.exp(col[128:] - line[:, :128]) * S.aff[sp, 128:, :128]
            br = jnp.exp(jnp.where(lower, col[128:] - line[:, 128:], NEG)) * S.aff[sp, 128:, 128:]
            mine = values * lane_masks[u]
            top += mm(tl.astype(BF16), mine[:128])
            bottom += mm(jnp.concatenate([bl.astype(BF16), br.astype(BF16)], axis=1), mine)
        S.inner[at256(sp, 128), lanes] = top
        S.inner[at128(2 * sp + 1), lanes] = bottom
        return carry

    lax.fori_loop(0, 16, within_span, 0)

    lax.fori_loop(1, 8, lambda i, carry: (load_w((z + i) % 8).wait(), carry)[1], 0)
    for dist in (1, 2, 3):
        d_chip_copy(dist).wait_recv()
    ring_step(0)

    exchange_3(0)
    exchange_4(0)
    for half in (0, 1):
        S.ent[0, half] = S.inc[0, half].astype(BF16)
        S.ent[1, half] = (
            jnp.exp(S.tots[0, half, 0:1, :]) * S.inc[0, half] + S.adds[0, half]
        ).astype(BF16)

    def scan_rows(it, carry):
        sp, hp, rows, lanes, half, half_lanes = where_of(it)
        carried = mm(S.cv[rows, :], S.ent[sp, half, :, half_lanes])
        value = S.inner[rows, lanes] + jnp.exp(pair_log(rows, hp)) * carried
        S.scan_t[lanes, rows] = value.T.astype(BF16)
        return carry

    lax.fori_loop(0, 16, scan_rows, 0)
    scan_copy = remote(S.scan_t, S.scan_t_sib, S.scan_s_sem.at[0], S.scan_r_sem.at[0], sib)
    scan_copy.start()

    def block_of(b):
        d = (b + 1) // 2
        return (z + jnp.where(b % 2 == 1, 8 - d, d)) % 8

    def xa_copy(k, j):
        to = 2 * (k % 2) + j
        slot = (x + 4 - to) % 4 - 1
        return to, remote(
            S.part.at[k, pl.ds(0, 512), pl.ds(j * 128, 128)],
            S.xa_in.at[k // 2, slot],
            S.xa_s_sem.at[k * 2 + j],
            S.xa_r_sem.at[(k // 2) * 3 + slot],
            x_peer(to),
        )

    def ya_copy(k):
        to = k // 2
        slot = (y + 4 - to) % 4 - 1
        return to, remote(
            S.part.at[k, pl.ds(512, 512)],
            S.ya_in.at[k % 2, slot],
            S.ya_s_sem.at[k],
            S.ya_r_sem.at[(k % 2) * 3 + slot],
            y_peer(to),
        )

    def xb_copy(k):
        to = k // 2
        slot = (y + 4 - to) % 4 - 1
        return to, remote(
            S.xq.at[to], S.xb_in.at[slot], S.xb_s_sem.at[to], S.xb_r_sem.at[slot], y_peer(to)
        )

    def yb_copy(k, j):
        to = 2 * (k % 2) + j
        slot = (x + 4 - to) % 4 - 1
        return to, remote(
            S.yq.at[k % 2, :, pl.ds(j * 128, 128)],
            S.yb_in.at[slot],
            S.yb_s_sem.at[to],
            S.yb_r_sem.at[slot],
            x_peer(to),
        )

    def weight_part(b, carry):
        k = block_of(b)
        for half in (0, 1):
            for copy in sib_columns(k, half):
                copy.wait_recv()

        def tile(m, inner_carry):
            rows = at256(m)
            mine = jnp.concatenate(
                [S.cot[k, :, at128(c)], S.cot[k, :, at128(2 + c)]], axis=1
            )
            total = mm(S.scan_t[rows, :], mine) + mm(S.scan_t_sib[rows, :], S.cot_sib[k])
            S.part[k, rows, :] = total.astype(BF16)
            return inner_carry

        lax.fori_loop(0, 4, tile, 0)
        for j in (0, 1):
            to, copy = xa_copy(k, j)
            pl.when(to != x)(copy.start)
        to, copy = ya_copy(k)
        pl.when(to != y)(copy.start)
        return carry

    def wait_in(buffer, sem):
        remote(buffer, buffer, sem, sem, sib).wait_recv()

    def weight_turn(b, carry):
        k = block_of(b)
        yk = k // 2
        kx = k % 2

        @pl.when(x // 2 == kx)
        def _():
            for i in (0, 1, 2):
                wait_in(S.xa_in.at[yk, i], S.xa_r_sem.at[yk * 3 + i])
            total = S.part[k, pl.ds(0, 512), at128(x % 2)].astype(F32)
            for i in (0, 1, 2):
                total = total + S.xa_in[yk, i].astype(F32)
            S.xq[yk] = total.astype(BF16)
            to, copy = xb_copy(k)
            pl.when(to != y)(copy.start)

        @pl.when(yk == y)
        def _():
            for i in (0, 1, 2):
                wait_in(S.ya_in.at[kx, i], S.ya_r_sem.at[kx * 3 + i])
            for j in (0, 1):
                cols = pl.ds(j * 128, 128)
                total = S.part[k, pl.ds(512, 512), cols].astype(F32)
                for i in (0, 1, 2):
                    total = total + S.ya_in[kx, i, :, cols].astype(F32)
                S.yq[kx, :, cols] = total.astype(BF16)
                to, copy = yb_copy(k, j)
                pl.when(to != x)(copy.start)

        return carry

    def turned_weights(it, carry):
        sp, hp, rows, lanes, half, half_lanes = where_of(it)
        for u in (0, 1):
            i = sp * 16 + 2 * hp + u
            col = S.la[2 * hp + u, rows, :]
            line = S.la_row[i, 0:1, :]
            tl = jnp.exp(jnp.where(upper, line[:, :128] - col[:128], NEG))
            tr = jnp.exp(line[:, 128:] - col[:128])
            br = jnp.exp(jnp.where(upper, line[:, 128:] - col[128:], NEG))
            S.within_t[i, 0] = tl.astype(BF16)
            S.within_t[i, 1] = tr.astype(BF16)
            S.within_t[i, 2] = br.astype(BF16)
            S.weights_t[i, 0] = (tl * S.aff_t[sp, :128, :128]).astype(BF16)
            S.weights_t[i, 1] = (tr * S.aff_t[sp, :128, 128:]).astype(BF16)
            S.weights_t[i, 2] = (br * S.aff_t[sp, 128:, 128:]).astype(BF16)
        return carry

    scan_copy.wait_recv()

    def ring_pair(i, carry):
        ring_step(2 * i + 1)
        lax.fori_loop(jnp.where(i == 0, 0, 2 * i + 1), 2 * i + 3, weight_part, 0)
        lax.fori_loop(6 * i, jnp.minimum(6 * i + 6, 16), turned_weights, 0)
        ring_step(2 * i + 2)
        low = jnp.where(i == 0, 0, jnp.where(i == 1, 3, 5))
        high = jnp.where(i == 0, 3, 5)
        lax.fori_loop(low, high, weight_turn, 0)
        return carry

    lax.fori_loop(0, 3, ring_pair, 0)

    def pull(it, carry):
        sp, hp, rows, lanes, half, half_lanes = where_of(it)
        grad = S.y_acc[rows, lanes].astype(BF16)
        S.gy[rows, lanes] = grad
        scaled = (jnp.exp(pair_log(rows, hp)) * grad.astype(F32)).astype(BF16)
        S.gy_start[rows, lanes] = scaled
        S.adds[sp, half, :, half_lanes] = mm(S.c_t[sp], scaled)
        return carry

    lax.fori_loop(0, 16, pull, 0)
    for half in (0, 1):
        S.loc[1, half] = S.adds[0, half] + jnp.exp(S.tots[0, half, 0:1, :]) * S.adds[1, half]
    exchange_1(1)
    weight_part(7, 0)
    exchange_2(1)
    lax.fori_loop(5, 7, weight_turn, 0)

    def within_back(it, carry):
        sp, hp, rows, lanes, half, half_lanes = where_of(it)
        values = S.xv[rows, lanes]
        grads = S.gy[rows, lanes]
        top = jnp.zeros((128, 128), F32)
        bottom = jnp.zeros((128, 128), F32)
        tl = jnp.zeros((128, 128), F32)
        tr = jnp.zeros((128, 128), F32)
        br = jnp.zeros((128, 128), F32)
        for u in (0, 1):
            i = sp * 16 + 2 * hp + u
            mine = values * lane_masks[u]
            grad = grads * lane_masks[u]
            pair_top = mm_nt(mine[:128], grads)
            pair_bottom = mm_nt(mine[128:], grads[128:])
            tl += pair_top[:, :128] * S.within_t[i, 0].astype(F32)
            tr += pair_top[:, 128:] * S.within_t[i, 1].astype(F32)
            br += pair_bottom * S.within_t[i, 2].astype(F32)
            top += mm(jnp.concatenate([S.weights_t[i, 0], S.weights_t[i, 1]], axis=1), grad)
            bottom += mm(S.weights_t[i, 2], grad[128:])
        S.inner[at256(sp, 128), lanes] = top
        S.inner[at128(2 * sp + 1), lanes] = bottom
        S.aff_grad[sp, :128, :128] += tl
        S.aff_grad[sp, :128, 128:] += tr
        S.aff_grad[sp, 128:, 128:] += br
        return carry

    S.aff_grad[...] = jnp.zeros_like(S.aff_grad)
    lax.fori_loop(0, 16, within_back, 0)

    for sp in (0, 1):
        rows = pl.ds(sp * 256, 256)
        grad = mm_nt(S.gy_start[rows, :512], S.ent[sp, 0]) + mm_nt(S.gy_start[rows, 512:], S.ent[sp, 1])
        tl = S.aff_grad[sp, :128, :128].T.astype(BF16)
        tr = S.aff_grad[sp, :128, 128:].T.astype(BF16)
        br = S.aff_grad[sp, 128:, 128:].T.astype(BF16)
        writes = S.bv[rows, :]
        S.c_out[pl.ds(sp * 256, 128), :] = (grad[:128] + mm(tl, writes[:128])).astype(BF16)
        S.c_out[pl.ds(sp * 256 + 128, 128), :] = (
            grad[128:] + mm(jnp.concatenate([tr, br], axis=1), writes)
        ).astype(BF16)
    store_c = pltpu.make_async_copy(S.c_out, cg_hbm.at[0], S.store_sem.at[0])
    store_c.start()

    exchange_3(1)
    weight_turn(7, 0)
    exchange_4(1)
    for half in (0, 1):
        S.lv[1, half] = S.inc[1, half].astype(BF16)
        S.lv[0, half] = (
            S.adds[1, half] + jnp.exp(S.tots[1, half, 0:1, :]) * S.inc[1, half]
        ).astype(BF16)

    def x_final(it, carry):
        sp, hp, rows, lanes, half, half_lanes = where_of(it)
        logs = pair_log(rows, hp)
        to_end = jnp.exp(logs[255:256, :] - logs)
        late = mm(S.bv[rows, :], S.lv[sp, half, :, half_lanes])
        S.x_out[rows, lanes] = (S.inner[rows, lanes] + to_end * late).astype(BF16)
        return carry

    lax.fori_loop(0, 16, x_final, 0)
    store_x = pltpu.make_async_copy(S.x_out, xg_hbm.at[0], S.store_sem.at[1])
    store_x.start()

    for sp in (0, 1):
        rows = pl.ds(sp * 256, 256)
        grad = mm_nt(S.x_end[rows, :512], S.lv[sp, 0]) + mm_nt(S.x_end[rows, 512:], S.lv[sp, 1])
        top = S.aff_grad[sp, :128, :].astype(BF16)
        br = S.aff_grad[sp, 128:, 128:].astype(BF16)
        reads = S.cv[rows, :]
        S.b_out[pl.ds(sp * 256, 128), :] = (grad[:128] + mm(top, reads)).astype(BF16)
        S.b_out[pl.ds(sp * 256 + 128, 128), :] = (grad[128:] + mm(br, reads[128:])).astype(BF16)
    store_b = pltpu.make_async_copy(S.b_out, bg_hbm.at[0], S.store_sem.at[2])
    store_b.start()

    for i in (0, 1, 2):
        wait_in(S.xb_in.at[i], S.xb_r_sem.at[i])
    total = S.xq[y].astype(F32)
    for i in (0, 1, 2):
        total = total + S.xb_in[i].astype(F32)
    S.w_out[pl.ds(0, 512), :] = total.astype(BF16)
    for i in (0, 1, 2):
        wait_in(S.yb_in.at[i], S.yb_r_sem.at[i])
    total = S.yq[x // 2, :, at128(x % 2)].astype(F32)
    for i in (0, 1, 2):
        total = total + S.yb_in[i].astype(F32)
    S.w_out[pl.ds(512, 512), :] = total.astype(BF16)
    store_w = pltpu.make_async_copy(S.w_out, wg_hbm, S.store_sem.at[3])
    store_w.start()

    def ring_sent(u, carry):
        for copy in ring(u, z, z):
            copy.wait_send()
        return carry

    lax.fori_loop(0, 7, ring_sent, 0)

    def block_sent(k, carry):
        for half in (0, 1):
            for copy in sib_columns(k, half):
                copy.wait_send()
        for j in (0, 1):
            to, copy = xa_copy(k, j)
            pl.when(to != x)(copy.wait_send)
        to, copy = ya_copy(k)
        pl.when(to != y)(copy.wait_send)

        @pl.when(x // 2 == k % 2)
        def _():
            to, copy = xb_copy(k)
            pl.when(to != y)(copy.wait_send)

        @pl.when(k // 2 == y)
        def _():
            for j in (0, 1):
                to, copy = yb_copy(k, j)
                pl.when(to != x)(copy.wait_send)

        return carry

    lax.fori_loop(0, 8, block_sent, 0)
    scan_copy.wait_send()
    d_sib_copy().wait_send()
    for dist in (1, 2, 3):
        d_chip_copy(dist).wait_send()
    for way in (0, 1):
        l1_copy(way).wait_send()
        l3_copy(way).wait_send()
        core, chip = place_of(way)
        for dist in (1, 2, 3):

            @pl.when(chip + dist <= 3)
            def _():
                l2_copy(way, dist).wait_send()

    for store in (store_c, store_x, store_b, store_w):
        store.wait()


def per_device(x_in, b_in, c_in, log_decay, out_weight, out_grad):
    out_shape = (
        jax.ShapeDtypeStruct((1024, 128), BF16),
        jax.ShapeDtypeStruct((1, 512, 1024), BF16),
        jax.ShapeDtypeStruct((1, 512, 128), BF16),
        jax.ShapeDtypeStruct((1, 512, 128), BF16),
    )
    scratch = [pltpu.VMEM(shape, dtype) for shape, dtype in VMEM_SCRATCH.values()]
    scratch += [pltpu.SemaphoreType.DMA(shape) for shape in SEMAPHORES.values()]
    return pl.pallas_call(
        kernel,
        out_shape=out_shape,
        in_specs=[pl.BlockSpec(memory_space=pl.ANY)] * 6,
        out_specs=[pl.BlockSpec(memory_space=pl.ANY)] * 4,
        scratch_shapes=scratch,
        compiler_params=pltpu.CompilerParams(
            collective_id=0, has_side_effects=True, vmem_limit_bytes=63 * 2**20
        ),
    )(x_in, b_in, c_in, log_decay, out_weight, out_grad)


def solution(mesh):
    in_specs = (
        P("dp", "seq", "tensor"),
        P("dp", "seq", "tensor"),
        P("dp", "seq", "tensor"),
        P("dp", "seq", "tensor"),
        P("tensor", None),
        P("dp", "seq", "tensor"),
    )
    out_specs = (
        P("tensor", ("dp", "seq")),
        P("dp", "seq", "tensor"),
        P("dp", "seq", "tensor"),
        P("dp", "seq", "tensor"),
    )
    return jax.shard_map(
        per_device, mesh=mesh, in_specs=in_specs, out_specs=out_specs, check_vma=False
    )
```

```python
from types import SimpleNamespace

import jax
import jax.numpy as jnp
from jax import lax
from jax.experimental import pallas as pl
from jax.experimental.pallas import tpu as pltpu
from jax.sharding import PartitionSpec as P

F32 = jnp.float32
BF16 = jnp.bfloat16
MESH = pl.DeviceIdType.MESH
NEG = -1e30
X_ROWS = 640
Y_ROWS = 1024 - X_ROWS

VMEM_SCRATCH = dict(
    xv=((512, 1024), BF16),
    bv=((512, 128), BF16),
    cv=((512, 128), BF16),
    dv=((128, 512), F32),
    wv=((8, 1024, 512), BF16),
    cot=((8, 512, 512), BF16),
    cot_sib=((8, 512, 256), BF16),
    b_t=((2, 128, 256), BF16),
    c_t=((2, 128, 256), BF16),
    la=((16, 512, 128), F32),
    la_row=((32, 8, 256), F32),
    tots=((2, 2, 8, 512), F32),
    aff=((2, 256, 256), F32),
    aff_t=((2, 256, 256), F32),
    within_t=((32, 3, 128, 128), BF16),
    weights_t=((32, 3, 128, 128), BF16),
    x_end=((512, 1024), BF16),
    inner=((512, 1024), F32),
    y_acc=((512, 1024), F32),
    gy=((512, 1024), BF16),
    gy_start=((512, 1024), BF16),
    scan_t=((1024, 512), BF16),
    scan_t_sib=((1024, 512), BF16),
    adds=((2, 2, 128, 512), F32),
    loc=((2, 2, 128, 512), F32),
    inc=((2, 2, 128, 512), F32),
    inh=((128, 512), F32),
    ent=((2, 2, 128, 512), BF16),
    lv=((2, 2, 128, 512), BF16),
    l1_out=((2, 2, 128, 512), BF16),
    l1_in=((2, 128, 512), BF16),
    l2_out=((2, 128, 512), BF16),
    l2_in=((2, 3, 128, 512), BF16),
    l3_out=((2, 128, 512), BF16),
    l3_in=((2, 128, 512), BF16),
    d_own=((2, 8, 512), F32),
    d_sib=((8, 512), F32),
    d_chip=((4, 8, 512), F32),
    part=((8, 1024, 256), BF16),
    xa_in=((4, 3, X_ROWS, 128), BF16),
    ya_in=((2, 3, Y_ROWS, 256), BF16),
    xq=((4, X_ROWS, 128), BF16),
    yq=((2, Y_ROWS, 256), BF16),
    xb_in=((3, X_ROWS, 128), BF16),
    yb_in=((3, Y_ROWS, 128), BF16),
    aff_grad=((2, 256, 256), F32),
    x_out=((512, 1024), BF16),
    b_out=((512, 128), BF16),
    c_out=((512, 128), BF16),
    w_out=((1024, 128), BF16),
)
SEMAPHORES = dict(
    load=(6,),
    load_w=(8,),
    right_s=(7,),
    right_r=(7,),
    left_s=(7,),
    left_r=(7,),
    sib_s=(32,),
    sib_r=(32,),
    scan_s=(1,),
    scan_r=(1,),
    ds_s=(1,),
    ds_r=(1,),
    dc_s=(4,),
    dc_r=(4,),
    l1_s=(2,),
    l1_r=(2,),
    l2_s=(6,),
    l2_r=(6,),
    l3_s=(2,),
    l3_r=(2,),
    xa_s=(16,),
    xa_r=(12,),
    ya_s=(8,),
    ya_r=(6,),
    xb_s=(4,),
    xb_r=(3,),
    yb_s=(4,),
    yb_r=(3,),
    store=(4,),
)
NAMES = list(VMEM_SCRATCH) + [f"{n}_sem" for n in SEMAPHORES]


def mm(a, b):
    return jnp.dot(a, b, preferred_element_type=F32)


def mm_nt(a, b):
    return lax.dot_general(a, b, (((1,), (1,)), ((), ())), preferred_element_type=F32)


def at128(i, size=128):
    return pl.ds(pl.multiple_of(i * 128, 128), size)


def at256(i, size=256):
    return pl.ds(pl.multiple_of(i * 256, 256), size)


def split3(v):
    hi = v.astype(BF16)
    rest = v - hi.astype(F32)
    mid = rest.astype(BF16)
    return hi, mid, (rest - mid.astype(F32)).astype(BF16)


def kernel(x_hbm, b_hbm, c_hbm, d_hbm, w_hbm, g_hbm, wg_hbm, xg_hbm, bg_hbm, cg_hbm, *scratch):
    S = SimpleNamespace(**dict(zip(NAMES, scratch)))
    y = lax.axis_index("dp")
    s = lax.axis_index("seq")
    z = lax.axis_index("tensor")
    x = s // 2
    c = s % 2
    sib = (y, x * 2 + (1 - c), z)
    right = (y, s, (z + 1) % 8)
    left = (y, s, (z + 7) % 8)

    def x_peer(xx):
        return (y, xx * 2 + c, z)

    def y_peer(yy):
        return (yy, s, z)

    def remote(src, dst, send_sem, recv_sem, device):
        return pltpu.make_async_remote_copy(
            src_ref=src,
            dst_ref=dst,
            send_sem=send_sem,
            recv_sem=recv_sem,
            device_id=device,
            device_id_type=MESH,
        )

    loads = [
        pltpu.make_async_copy(d_hbm.at[0], S.dv.at[pl.ds(0, 16)], S.load_sem.at[0]),
        pltpu.make_async_copy(b_hbm.at[0], S.bv, S.load_sem.at[1]),
        pltpu.make_async_copy(c_hbm.at[0], S.cv, S.load_sem.at[2]),
        pltpu.make_async_copy(x_hbm.at[0], S.xv, S.load_sem.at[3]),
        pltpu.make_async_copy(g_hbm.at[0], S.cot.at[z], S.load_sem.at[4]),
    ]
    for load in loads:
        load.start()

    def load_w(k):
        return pltpu.make_async_copy(
            w_hbm.at[:, pl.ds(pl.multiple_of(k * 512, 512), 512)], S.wv.at[k], S.load_w_sem.at[k]
        )

    load_w(z).start()

    barrier = pltpu.get_barrier_semaphore()
    peers = [sib, right, left]
    peers += [x_peer((x + i) % 4) for i in (1, 2, 3)] + [y_peer((y + i) % 4) for i in (1, 2, 3)]
    for peer in peers:
        pl.semaphore_signal(barrier, inc=1, device_id=peer, device_id_type=MESH)
    pl.semaphore_wait(barrier, len(peers))

    def ring(u, k_right, k_left, own=False):
        half_r = u % 2
        half_l = 1 - u % 2
        rows_r = at256(half_r)
        rows_l = at256(half_l)
        src_r = g_hbm.at[0, rows_r] if own else S.cot.at[k_right, rows_r]
        src_l = g_hbm.at[0, rows_l] if own else S.cot.at[k_left, rows_l]
        return (
            remote(src_r, S.cot.at[k_right, rows_r], S.right_s_sem.at[u], S.right_r_sem.at[u], right),
            remote(src_l, S.cot.at[k_left, rows_l], S.left_s_sem.at[u], S.left_r_sem.at[u], left),
        )

    for u in (0, 1):
        for copy in ring(u, z, z, own=True):
            copy.start()

    def start_w(i, carry):
        load_w((z + i) % 8).start()
        return carry

    lax.fori_loop(1, 8, start_w, 0)

    def sib_columns(k, half):
        copies = []
        for j in (0, 1):
            i = k * 4 + half * 2 + j
            copies.append(
                remote(
                    S.cot.at[k, at256(half), at128(2 * j + 1 - c)],
                    S.cot_sib.at[k, at256(half), pl.ds(j * 128, 128)],
                    S.sib_s_sem.at[i],
                    S.sib_r_sem.at[i],
                    sib,
                )
            )
        return copies

    def y_block(k, half, first=False):
        rows = at256(half)

        for n in range(4):
            cols = pl.ds(n * 256, 256)
            part = mm_nt(S.cot[k, rows, :], S.wv[k, cols, :])
            if first:
                S.y_acc[rows, cols] = part
            else:
                S.y_acc[rows, cols] += part

    def ring_step(t):
        d = t // 2 + 1
        k_right = (z + 8 - d) % 8
        k_left = (z + d) % 8
        for copy in ring(t, k_right, k_left):
            copy.wait_recv()

        @pl.when(t <= 4)
        def _():
            for copy in ring(t + 2, k_right, k_left):
                copy.start()

        for copy in sib_columns(k_right, t % 2) + sib_columns(k_left, 1 - t % 2):
            copy.start()
        y_block(k_right, t % 2)
        y_block(k_left, 1 - t % 2)

    def iota(shape, dim):
        return lax.broadcasted_iota(jnp.int32, shape, dim)

    low_lanes = iota((256, 128), 1) < 64
    lane_row = iota((1, 128), 1)
    lane_masks = [
        jnp.where(lane_row < 64, 1.0, 0.0).astype(BF16),
        jnp.where(lane_row < 64, 0.0, 1.0).astype(BF16),
    ]
    lower = iota((128, 128), 0) >= iota((128, 128), 1)
    upper = iota((128, 128), 1) >= iota((128, 128), 0)

    S.dv[16:, :] = jnp.zeros((112, 512), F32)
    loads[0].wait()
    tril = jnp.where(iota((256, 256), 0) >= iota((256, 256), 1), 1.0, 0.0).astype(BF16)
    for sp in (0, 1):
        rows = pl.ds(sp * 256, 256)
        parts = split3(S.dv[:, rows])
        running = sum(mm_nt(tril, p) for p in parts)
        for h in range(16):
            S.la[h, rows, :] = jnp.broadcast_to(running[:, h : h + 1], (256, 128))
        turned = sum(mm_nt(p[:16], tril) for p in parts)
        for h in range(16):
            S.la_row[sp * 16 + h] = jnp.broadcast_to(turned[h : h + 1, :], (8, 256))

    def pair_log(rows, hp):
        return jnp.where(low_lanes, S.la[2 * hp, rows, :], S.la[2 * hp + 1, rows, :])

    def where_of(it):
        sp = it // 8
        hp = it % 8
        return sp, hp, at256(sp), at128(hp), hp // 4, at128(hp % 4)

    for load in loads[1:4]:
        load.wait()
    for sp in (0, 1):
        rows = pl.ds(sp * 256, 256)
        S.b_t[sp] = S.bv[rows, :].astype(F32).T.astype(BF16)
        S.c_t[sp] = S.cv[rows, :].astype(F32).T.astype(BF16)

    def span_add(it, carry):
        sp, hp, rows, lanes, half, half_lanes = where_of(it)
        logs = pair_log(rows, hp)
        total = logs[255:256, :]
        S.tots[sp, half, :, half_lanes] = jnp.broadcast_to(total, (8, 128))
        scaled = (jnp.exp(total - logs) * S.xv[rows, lanes].astype(F32)).astype(BF16)
        S.x_end[rows, lanes] = scaled
        S.adds[sp, half, :, half_lanes] = mm(S.b_t[sp], scaled)
        return carry

    lax.fori_loop(0, 16, span_add, 0, unroll=8)

    def row(ref):
        return ref[0:1, :]

    def exchange_1(way):
        for half in (0, 1):
            S.l1_out[way, half] = S.loc[way, half].astype(BF16)
        l1_copy(way).start()

    def l1_copy(way):
        return remote(
            S.l1_out.at[way, 1 - c], S.l1_in.at[way], S.l1_s_sem.at[way], S.l1_r_sem.at[way], sib
        )

    def l2_copy(way, dist):
        to = x + dist if way == 0 else x - dist
        i = way * 3 + dist - 1
        return remote(
            S.l2_out.at[way],
            S.l2_in.at[way, dist - 1],
            S.l2_s_sem.at[i],
            S.l2_r_sem.at[i],
            x_peer(to),
        )

    def l3_copy(way):
        return remote(S.l3_out.at[way], S.l3_in.at[way], S.l3_s_sem.at[way], S.l3_r_sem.at[way], sib)

    def place_of(way):
        return (c, x) if way == 0 else (1 - c, 3 - x)

    def exchange_2(way):
        core, chip = place_of(way)
        l1_copy(way).wait_recv()
        one = jnp.ones((1, 512), F32)
        a = jnp.where(core == 0, jnp.exp(row(S.d_sib)), one)
        b = jnp.where(core == 0, one, jnp.exp(S.d_own[c, 0:1, :]))
        S.l2_out[way] = (a * S.loc[way, c] + b * S.l1_in[way].astype(F32)).astype(BF16)
        for dist in (1, 2, 3):

            @pl.when(chip + dist <= 3)
            def _():
                l2_copy(way, dist).start()

    def exchange_3(way):
        core, chip = place_of(way)
        S.inh[...] = jnp.zeros_like(S.inh)
        near = 3 if way == 0 else 1
        for dist in (1, 2, 3):

            @pl.when(chip >= dist)
            def _():
                l2_copy(way, dist).wait_recv()
                term = S.l2_in[way, dist - 1].astype(F32)
                if dist == 2:
                    term = term * jnp.exp(S.d_chip[near, 0:1, :])
                if dist == 3:
                    term = term * jnp.exp(S.d_chip[near, 0:1, :] + S.d_chip[2, 0:1, :])
                S.inh[...] += term

        into = S.inh[...]
        own = S.loc[way, c] + jnp.exp(S.d_own[c, 0:1, :]) * into
        S.l3_out[way] = jnp.where(core == 0, own, into).astype(BF16)
        l3_copy(way).start()
        other = S.l1_in[way].astype(F32) + jnp.exp(row(S.d_sib)) * into
        S.inc[way, c] = jnp.where(core == 0, into, other)

    def exchange_4(way):
        l3_copy(way).wait_recv()
        S.inc[way, 1 - c] = S.l3_in[way].astype(F32)

    def d_sib_copy():
        return remote(S.d_own.at[1 - c], S.d_sib, S.ds_s_sem.at[0], S.ds_r_sem.at[0], sib)

    def d_chip_copy(dist):
        return remote(
            S.d_chip.at[0],
            S.d_chip.at[4 - dist],
            S.dc_s_sem.at[dist],
            S.dc_r_sem.at[4 - dist],
            x_peer((x + dist) % 4),
        )

    for half in (0, 1):
        S.d_own[half] = S.tots[0, half] + S.tots[1, half]
        S.loc[0, half] = jnp.exp(S.tots[1, half, 0:1, :]) * S.adds[0, half] + S.adds[1, half]
    d_sib_copy().start()
    exchange_1(0)

    loads[4].wait()
    for half in (0, 1):
        for copy in sib_columns(z, half):
            copy.start()
    load_w(z).wait()
    for half in (0, 1):
        y_block(z, half, first=True)

    d_sib_copy().wait_recv()
    S.d_chip[0] = S.d_own[c] + S.d_sib[...]
    for dist in (1, 2, 3):
        d_chip_copy(dist).start()
    exchange_2(0)

    for sp in (0, 1):
        rows = pl.ds(sp * 256, 256)
        S.aff[sp] = mm_nt(S.cv[rows, :], S.bv[rows, :])
        S.aff_t[sp] = mm_nt(S.bv[rows, :], S.cv[rows, :])

    def within_span(it, carry):
        sp, hp, rows, lanes, half, half_lanes = where_of(it)
        values = S.xv[rows, lanes]
        top = jnp.zeros((128, 128), F32)
        bottom = jnp.zeros((128, 128), F32)
        for u in (0, 1):
            col = S.la[2 * hp + u, rows, :]
            line = S.la_row[sp * 16 + 2 * hp + u, 0:1, :]
            tl = jnp.exp(jnp.where(lower, col[:128] - line[:, :128], NEG)) * S.aff[sp, :128, :128]
            bl = jnp.exp(col[128:] - line[:, :128]) * S.aff[sp, 128:, :128]
            br = jnp.exp(jnp.where(lower, col[128:] - line[:, 128:], NEG)) * S.aff[sp, 128:, 128:]
            mine = values * lane_masks[u]
            top += mm(tl.astype(BF16), mine[:128])
            bottom += mm(jnp.concatenate([bl.astype(BF16), br.astype(BF16)], axis=1), mine)
        S.inner[at256(sp, 128), lanes] = top
        S.inner[at128(2 * sp + 1), lanes] = bottom
        return carry

    lax.fori_loop(0, 16, within_span, 0, unroll=8)

    lax.fori_loop(1, 8, lambda i, carry: (load_w((z + i) % 8).wait(), carry)[1], 0)
    for dist in (1, 2, 3):
        d_chip_copy(dist).wait_recv()
    ring_step(0)

    exchange_3(0)
    exchange_4(0)
    for half in (0, 1):
        S.ent[0, half] = S.inc[0, half].astype(BF16)
        S.ent[1, half] = (
            jnp.exp(S.tots[0, half, 0:1, :]) * S.inc[0, half] + S.adds[0, half]
        ).astype(BF16)

    def scan_rows(it, carry):
        sp, hp, rows, lanes, half, half_lanes = where_of(it)
        carried = mm(S.cv[rows, :], S.ent[sp, half, :, half_lanes])
        value = S.inner[rows, lanes] + jnp.exp(pair_log(rows, hp)) * carried
        S.scan_t[lanes, rows] = value.T.astype(BF16)
        return carry

    lax.fori_loop(0, 16, scan_rows, 0, unroll=8)
    scan_copy = remote(S.scan_t, S.scan_t_sib, S.scan_s_sem.at[0], S.scan_r_sem.at[0], sib)
    scan_copy.start()

    def block_of(b):
        d = (b + 1) // 2
        return (z + jnp.where(b % 2 == 1, 8 - d, d)) % 8

    def xa_copy(k, j):
        to = 2 * (k % 2) + j
        slot = (x + 4 - to) % 4 - 1
        return to, remote(
            S.part.at[k, pl.ds(0, X_ROWS), pl.ds(j * 128, 128)],
            S.xa_in.at[k // 2, slot],
            S.xa_s_sem.at[k * 2 + j],
            S.xa_r_sem.at[(k // 2) * 3 + slot],
            x_peer(to),
        )

    def ya_copy(k):
        to = k // 2
        slot = (y + 4 - to) % 4 - 1
        return to, remote(
            S.part.at[k, pl.ds(X_ROWS, Y_ROWS)],
            S.ya_in.at[k % 2, slot],
            S.ya_s_sem.at[k],
            S.ya_r_sem.at[(k % 2) * 3 + slot],
            y_peer(to),
        )

    def xb_copy(k):
        to = k // 2
        slot = (y + 4 - to) % 4 - 1
        return to, remote(
            S.xq.at[to], S.xb_in.at[slot], S.xb_s_sem.at[to], S.xb_r_sem.at[slot], y_peer(to)
        )

    def yb_copy(k, j):
        to = 2 * (k % 2) + j
        slot = (x + 4 - to) % 4 - 1
        return to, remote(
            S.yq.at[k % 2, :, pl.ds(j * 128, 128)],
            S.yb_in.at[slot],
            S.yb_s_sem.at[to],
            S.yb_r_sem.at[slot],
            x_peer(to),
        )

    def weight_part(b, carry):
        k = block_of(b)
        for half in (0, 1):
            for copy in sib_columns(k, half):
                copy.wait_recv()

        for m in range(4):
            rows = pl.ds(m * 256, 256)
            mine = jnp.concatenate(
                [S.cot[k, :, at128(c)], S.cot[k, :, at128(2 + c)]], axis=1
            )
            total = mm(S.scan_t[rows, :], mine) + mm(S.scan_t_sib[rows, :], S.cot_sib[k])
            S.part[k, rows, :] = total.astype(BF16)
        for j in (0, 1):
            to, copy = xa_copy(k, j)
            pl.when(to != x)(copy.start)
        to, copy = ya_copy(k)
        pl.when(to != y)(copy.start)
        return carry

    def wait_in(buffer, sem):
        remote(buffer, buffer, sem, sem, sib).wait_recv()

    def weight_turn(b, carry):
        k = block_of(b)
        yk = k // 2
        kx = k % 2

        @pl.when(x // 2 == kx)
        def _():
            for i in (0, 1, 2):
                wait_in(S.xa_in.at[yk, i], S.xa_r_sem.at[yk * 3 + i])
            total = S.part[k, pl.ds(0, X_ROWS), at128(x % 2)].astype(F32)
            for i in (0, 1, 2):
                total = total + S.xa_in[yk, i].astype(F32)
            S.xq[yk] = total.astype(BF16)
            to, copy = xb_copy(k)
            pl.when(to != y)(copy.start)

        @pl.when(yk == y)
        def _():
            for i in (0, 1, 2):
                wait_in(S.ya_in.at[kx, i], S.ya_r_sem.at[kx * 3 + i])
            for j in (0, 1):
                cols = pl.ds(j * 128, 128)
                total = S.part[k, pl.ds(X_ROWS, Y_ROWS), cols].astype(F32)
                for i in (0, 1, 2):
                    total = total + S.ya_in[kx, i, :, cols].astype(F32)
                S.yq[kx, :, cols] = total.astype(BF16)
                to, copy = yb_copy(k, j)
                pl.when(to != x)(copy.start)

        return carry

    def turned_weights(it, carry):
        sp, hp, rows, lanes, half, half_lanes = where_of(it)
        for u in (0, 1):
            i = sp * 16 + 2 * hp + u
            col = S.la[2 * hp + u, rows, :]
            line = S.la_row[i, 0:1, :]
            tl = jnp.exp(jnp.where(upper, line[:, :128] - col[:128], NEG))
            tr = jnp.exp(line[:, 128:] - col[:128])
            br = jnp.exp(jnp.where(upper, line[:, 128:] - col[128:], NEG))
            S.within_t[i, 0] = tl.astype(BF16)
            S.within_t[i, 1] = tr.astype(BF16)
            S.within_t[i, 2] = br.astype(BF16)
            S.weights_t[i, 0] = (tl * S.aff_t[sp, :128, :128]).astype(BF16)
            S.weights_t[i, 1] = (tr * S.aff_t[sp, :128, 128:]).astype(BF16)
            S.weights_t[i, 2] = (br * S.aff_t[sp, 128:, 128:]).astype(BF16)
        return carry

    scan_copy.wait_recv()

    def ring_pair(i, carry):
        ring_step(2 * i + 1)
        lax.fori_loop(jnp.where(i == 0, 0, 2 * i + 1), 2 * i + 3, weight_part, 0)
        lax.fori_loop(6 * i, jnp.minimum(6 * i + 6, 16), turned_weights, 0)
        lax.fori_loop(1, jnp.where(i == 2, 3, 1), weight_turn, 0)
        ring_step(2 * i + 2)
        lax.fori_loop(0, jnp.where(i == 1, 1, 0), weight_turn, 0)
        return carry

    lax.fori_loop(0, 3, ring_pair, 0)

    def pull(it, carry):
        sp, hp, rows, lanes, half, half_lanes = where_of(it)
        grad = S.y_acc[rows, lanes].astype(BF16)
        S.gy[rows, lanes] = grad
        scaled = (jnp.exp(pair_log(rows, hp)) * grad.astype(F32)).astype(BF16)
        S.gy_start[rows, lanes] = scaled
        S.adds[sp, half, :, half_lanes] = mm(S.c_t[sp], scaled)
        return carry

    lax.fori_loop(0, 16, pull, 0, unroll=8)
    for half in (0, 1):
        S.loc[1, half] = S.adds[0, half] + jnp.exp(S.tots[0, half, 0:1, :]) * S.adds[1, half]
    exchange_1(1)
    weight_part(7, 0)
    exchange_2(1)
    lax.fori_loop(3, 5, weight_turn, 0)

    def within_back(it, carry):
        sp, hp, rows, lanes, half, half_lanes = where_of(it)
        values = S.xv[rows, lanes]
        grads = S.gy[rows, lanes]
        top = jnp.zeros((128, 128), F32)
        bottom = jnp.zeros((128, 128), F32)
        tl = jnp.zeros((128, 128), F32)
        tr = jnp.zeros((128, 128), F32)
        br = jnp.zeros((128, 128), F32)
        for u in (0, 1):
            i = sp * 16 + 2 * hp + u
            mine = values * lane_masks[u]
            grad = grads * lane_masks[u]
            pair_top = mm_nt(mine[:128], grads)
            pair_bottom = mm_nt(mine[128:], grads[128:])
            tl += pair_top[:, :128] * S.within_t[i, 0].astype(F32)
            tr += pair_top[:, 128:] * S.within_t[i, 1].astype(F32)
            br += pair_bottom * S.within_t[i, 2].astype(F32)
            top += mm(jnp.concatenate([S.weights_t[i, 0], S.weights_t[i, 1]], axis=1), grad)
            bottom += mm(S.weights_t[i, 2], grad[128:])
        S.inner[at256(sp, 128), lanes] = top
        S.inner[at128(2 * sp + 1), lanes] = bottom
        S.aff_grad[sp, :128, :128] += tl
        S.aff_grad[sp, :128, 128:] += tr
        S.aff_grad[sp, 128:, 128:] += br
        return carry

    S.aff_grad[...] = jnp.zeros_like(S.aff_grad)
    lax.fori_loop(0, 16, within_back, 0, unroll=8)

    for sp in (0, 1):
        rows = pl.ds(sp * 256, 256)
        grad = mm_nt(S.gy_start[rows, :512], S.ent[sp, 0]) + mm_nt(S.gy_start[rows, 512:], S.ent[sp, 1])
        tl = S.aff_grad[sp, :128, :128].T.astype(BF16)
        tr = S.aff_grad[sp, :128, 128:].T.astype(BF16)
        br = S.aff_grad[sp, 128:, 128:].T.astype(BF16)
        writes = S.bv[rows, :]
        S.c_out[pl.ds(sp * 256, 128), :] = (grad[:128] + mm(tl, writes[:128])).astype(BF16)
        S.c_out[pl.ds(sp * 256 + 128, 128), :] = (
            grad[128:] + mm(jnp.concatenate([tr, br], axis=1), writes)
        ).astype(BF16)
    store_c = pltpu.make_async_copy(S.c_out, cg_hbm.at[0], S.store_sem.at[0])
    store_c.start()

    lax.fori_loop(5, 7, weight_turn, 0)
    exchange_3(1)
    weight_turn(7, 0)
    exchange_4(1)
    for half in (0, 1):
        S.lv[1, half] = S.inc[1, half].astype(BF16)
        S.lv[0, half] = (
            S.adds[1, half] + jnp.exp(S.tots[1, half, 0:1, :]) * S.inc[1, half]
        ).astype(BF16)

    def x_final(it, carry):
        sp, hp, rows, lanes, half, half_lanes = where_of(it)
        logs = pair_log(rows, hp)
        to_end = jnp.exp(logs[255:256, :] - logs)
        late = mm(S.bv[rows, :], S.lv[sp, half, :, half_lanes])
        S.x_out[rows, lanes] = (S.inner[rows, lanes] + to_end * late).astype(BF16)
        return carry

    lax.fori_loop(0, 16, x_final, 0, unroll=8)
    store_x = pltpu.make_async_copy(S.x_out, xg_hbm.at[0], S.store_sem.at[1])
    store_x.start()

    for sp in (0, 1):
        rows = pl.ds(sp * 256, 256)
        grad = mm_nt(S.x_end[rows, :512], S.lv[sp, 0]) + mm_nt(S.x_end[rows, 512:], S.lv[sp, 1])
        top = S.aff_grad[sp, :128, :].astype(BF16)
        br = S.aff_grad[sp, 128:, 128:].astype(BF16)
        reads = S.cv[rows, :]
        S.b_out[pl.ds(sp * 256, 128), :] = (grad[:128] + mm(top, reads)).astype(BF16)
        S.b_out[pl.ds(sp * 256 + 128, 128), :] = (grad[128:] + mm(br, reads[128:])).astype(BF16)
    store_b = pltpu.make_async_copy(S.b_out, bg_hbm.at[0], S.store_sem.at[2])
    store_b.start()

    for i in (0, 1, 2):
        wait_in(S.xb_in.at[i], S.xb_r_sem.at[i])
    total = S.xq[y].astype(F32)
    for i in (0, 1, 2):
        total = total + S.xb_in[i].astype(F32)
    S.w_out[pl.ds(0, X_ROWS), :] = total.astype(BF16)
    for i in (0, 1, 2):
        wait_in(S.yb_in.at[i], S.yb_r_sem.at[i])
    total = S.yq[x // 2, :, at128(x % 2)].astype(F32)
    for i in (0, 1, 2):
        total = total + S.yb_in[i].astype(F32)
    S.w_out[pl.ds(X_ROWS, Y_ROWS), :] = total.astype(BF16)
    store_w = pltpu.make_async_copy(S.w_out, wg_hbm, S.store_sem.at[3])
    store_w.start()

    def ring_sent(u, carry):
        for copy in ring(u, z, z):
            copy.wait_send()
        return carry

    lax.fori_loop(0, 7, ring_sent, 0)

    def block_sent(k, carry):
        for half in (0, 1):
            for copy in sib_columns(k, half):
                copy.wait_send()
        for j in (0, 1):
            to, copy = xa_copy(k, j)
            pl.when(to != x)(copy.wait_send)
        to, copy = ya_copy(k)
        pl.when(to != y)(copy.wait_send)

        @pl.when(x // 2 == k % 2)
        def _():
            to, copy = xb_copy(k)
            pl.when(to != y)(copy.wait_send)

        @pl.when(k // 2 == y)
        def _():
            for j in (0, 1):
                to, copy = yb_copy(k, j)
                pl.when(to != x)(copy.wait_send)

        return carry

    lax.fori_loop(0, 8, block_sent, 0)
    scan_copy.wait_send()
    d_sib_copy().wait_send()
    for dist in (1, 2, 3):
        d_chip_copy(dist).wait_send()
    for way in (0, 1):
        l1_copy(way).wait_send()
        l3_copy(way).wait_send()
        core, chip = place_of(way)
        for dist in (1, 2, 3):

            @pl.when(chip + dist <= 3)
            def _():
                l2_copy(way, dist).wait_send()

    for store in (store_c, store_x, store_b, store_w):
        store.wait()


def copy_kernel(*refs):
    ins, outs, held, sems = refs[:4], refs[4:8], refs[8:12], refs[12]
    pieces = []
    for n, (src, dst, mid) in enumerate(zip(ins, outs, held)):
        size = 256 if n else 512
        for i in range(1024 // size if n == 0 else 512 // size):
            rows = pl.ds(i * size, size)
            at = (rows,) if n == 0 else (0, rows)
            j = 2 * len(pieces)
            pieces.append(
                (
                    pltpu.make_async_copy(src.at[at], mid.at[at], sems.at[j]),
                    pltpu.make_async_copy(mid.at[at], dst.at[at], sems.at[j + 1]),
                )
            )
    for come, _ in pieces:
        come.start()
    for come, go in pieces:
        come.wait()
        go.start()
    for _, go in pieces:
        go.wait()


def per_device(x_in, b_in, c_in, log_decay, out_weight, out_grad):
    out_shape = (
        jax.ShapeDtypeStruct((1024, 128), BF16),
        jax.ShapeDtypeStruct((1, 512, 1024), BF16),
        jax.ShapeDtypeStruct((1, 512, 128), BF16),
        jax.ShapeDtypeStruct((1, 512, 128), BF16),
    )
    scratch = [pltpu.VMEM(shape, dtype) for shape, dtype in VMEM_SCRATCH.values()]
    scratch += [pltpu.SemaphoreType.DMA(shape) for shape in SEMAPHORES.values()]
    results = pl.pallas_call(
        kernel,
        out_shape=out_shape,
        in_specs=[pl.BlockSpec(memory_space=pl.ANY)] * 6,
        out_specs=[pl.BlockSpec(memory_space=pl.ANY)] * 4,
        scratch_shapes=scratch,
        compiler_params=pltpu.CompilerParams(
            collective_id=0, has_side_effects=True, vmem_limit_bytes=63 * 2**20
        ),
    )(x_in, b_in, c_in, jnp.transpose(log_decay, (0, 2, 1)), out_weight, out_grad)
    return pl.pallas_call(
        copy_kernel,
        out_shape=out_shape,
        in_specs=[pl.BlockSpec(memory_space=pl.ANY)] * 4,
        out_specs=[pl.BlockSpec(memory_space=pl.ANY)] * 4,
        scratch_shapes=[pltpu.VMEM(o.shape, o.dtype) for o in out_shape]
        + [pltpu.SemaphoreType.DMA((16,))],
    )(*results)


def solution(mesh):
    in_specs = (
        P("dp", "seq", "tensor"),
        P("dp", "seq", "tensor"),
        P("dp", "seq", "tensor"),
        P("dp", "seq", "tensor"),
        P("tensor", None),
        P("dp", "seq", "tensor"),
    )
    out_specs = (
        P("tensor", ("dp", "seq")),
        P("dp", "seq", "tensor"),
        P("dp", "seq", "tensor"),
        P("dp", "seq", "tensor"),
    )
    return jax.shard_map(
        per_device, mesh=mesh, in_specs=in_specs, out_specs=out_specs, check_vma=False
    )
```

```python
from types import SimpleNamespace

import jax
import jax.numpy as jnp
from jax import lax
from jax.experimental import pallas as pl
from jax.experimental.pallas import tpu as pltpu
from jax.sharding import PartitionSpec as P

F32 = jnp.float32
BF16 = jnp.bfloat16
MESH = pl.DeviceIdType.MESH
NEG = -1e30
X_ROWS = 608
Y_ROWS = 1024 - X_ROWS

VMEM_SCRATCH = dict(
    xv=((512, 1024), BF16),
    bv=((512, 128), BF16),
    cv=((512, 128), BF16),
    dv=((128, 512), F32),
    wv=((8, 1024, 512), BF16),
    cot=((8, 512, 512), BF16),
    cot_sib=((8, 512, 256), BF16),
    b_t=((2, 128, 256), BF16),
    c_t=((2, 128, 256), BF16),
    la=((16, 512, 128), F32),
    la_row=((32, 8, 256), F32),
    tots=((2, 2, 8, 512), F32),
    aff=((2, 256, 256), F32),
    aff_t=((2, 256, 256), F32),
    within_t=((32, 3, 128, 128), BF16),
    weights_t=((32, 3, 128, 128), BF16),
    x_end=((512, 1024), BF16),
    inner=((512, 1024), F32),
    y_acc=((512, 1024), F32),
    gy=((512, 1024), BF16),
    gy_start=((512, 1024), BF16),
    scan_t=((1024, 512), BF16),
    scan_t_sib=((1024, 512), BF16),
    adds=((2, 2, 128, 512), F32),
    loc=((2, 2, 128, 512), F32),
    inc=((2, 2, 128, 512), F32),
    inh=((128, 512), F32),
    ent=((2, 2, 128, 512), BF16),
    lv=((2, 2, 128, 512), BF16),
    l1_out=((2, 2, 128, 512), BF16),
    l1_in=((2, 128, 512), BF16),
    l2_out=((2, 128, 512), BF16),
    l2_in=((2, 3, 128, 512), BF16),
    l3_out=((2, 128, 512), BF16),
    l3_in=((2, 128, 512), BF16),
    d_own=((2, 8, 512), F32),
    d_sib=((8, 512), F32),
    d_chip=((4, 8, 512), F32),
    part=((8, 1024, 256), BF16),
    xa_in=((4, 3, X_ROWS, 128), BF16),
    ya_in=((2, 3, Y_ROWS, 256), BF16),
    xq=((4, X_ROWS, 128), BF16),
    yq=((2, Y_ROWS, 256), BF16),
    xb_in=((3, X_ROWS, 128), BF16),
    yb_in=((3, Y_ROWS, 128), BF16),
    aff_grad=((2, 256, 256), F32),
    x_out=((512, 1024), BF16),
    b_out=((512, 128), BF16),
    c_out=((512, 128), BF16),
    w_out=((1024, 128), BF16),
)
SEMAPHORES = dict(
    load=(6,),
    load_w=(8,),
    right_s=(7,),
    right_r=(7,),
    left_s=(7,),
    left_r=(7,),
    sib_s=(32,),
    sib_r=(32,),
    scan_s=(1,),
    scan_r=(1,),
    ds_s=(1,),
    ds_r=(1,),
    dc_s=(4,),
    dc_r=(4,),
    l1_s=(2,),
    l1_r=(2,),
    l2_s=(6,),
    l2_r=(6,),
    l3_s=(2,),
    l3_r=(2,),
    xa_s=(16,),
    xa_r=(12,),
    ya_s=(8,),
    ya_r=(6,),
    xb_s=(4,),
    xb_r=(3,),
    yb_s=(4,),
    yb_r=(3,),
    store=(4,),
)
NAMES = list(VMEM_SCRATCH) + [f"{n}_sem" for n in SEMAPHORES]


def mm(a, b):
    return jnp.dot(a, b, preferred_element_type=F32)


def mm_nt(a, b):
    return lax.dot_general(a, b, (((1,), (1,)), ((), ())), preferred_element_type=F32)


def at128(i, size=128):
    return pl.ds(pl.multiple_of(i * 128, 128), size)


def at256(i, size=256):
    return pl.ds(pl.multiple_of(i * 256, 256), size)


def split3(v):
    hi = v.astype(BF16)
    rest = v - hi.astype(F32)
    mid = rest.astype(BF16)
    return hi, mid, (rest - mid.astype(F32)).astype(BF16)


def kernel(x_hbm, b_hbm, c_hbm, d_hbm, w_hbm, g_hbm, wg_hbm, xg_hbm, bg_hbm, cg_hbm, *scratch):
    S = SimpleNamespace(**dict(zip(NAMES, scratch)))
    y = lax.axis_index("dp")
    s = lax.axis_index("seq")
    z = lax.axis_index("tensor")
    x = s // 2
    c = s % 2
    sib = (y, x * 2 + (1 - c), z)
    right = (y, s, (z + 1) % 8)
    left = (y, s, (z + 7) % 8)

    def x_peer(xx):
        return (y, xx * 2 + c, z)

    def y_peer(yy):
        return (yy, s, z)

    def remote(src, dst, send_sem, recv_sem, device):
        return pltpu.make_async_remote_copy(
            src_ref=src,
            dst_ref=dst,
            send_sem=send_sem,
            recv_sem=recv_sem,
            device_id=device,
            device_id_type=MESH,
        )

    loads = [
        pltpu.make_async_copy(d_hbm.at[0], S.dv.at[pl.ds(0, 16)], S.load_sem.at[0]),
        pltpu.make_async_copy(b_hbm.at[0], S.bv, S.load_sem.at[1]),
        pltpu.make_async_copy(c_hbm.at[0], S.cv, S.load_sem.at[2]),
        pltpu.make_async_copy(x_hbm.at[0], S.xv, S.load_sem.at[3]),
        pltpu.make_async_copy(g_hbm.at[0], S.cot.at[z], S.load_sem.at[4]),
    ]
    for load in loads:
        load.start()

    def load_w(k):
        return pltpu.make_async_copy(
            w_hbm.at[:, pl.ds(pl.multiple_of(k * 512, 512), 512)], S.wv.at[k], S.load_w_sem.at[k]
        )

    load_w(z).start()

    barrier = pltpu.get_barrier_semaphore()
    peers = [sib, right, left]
    peers += [x_peer((x + i) % 4) for i in (1, 2, 3)] + [y_peer((y + i) % 4) for i in (1, 2, 3)]
    for peer in peers:
        pl.semaphore_signal(barrier, inc=1, device_id=peer, device_id_type=MESH)
    pl.semaphore_wait(barrier, len(peers))

    def ring(u, k_right, k_left, own=False):
        half_r = u % 2
        half_l = 1 - u % 2
        rows_r = at256(half_r)
        rows_l = at256(half_l)
        src_r = g_hbm.at[0, rows_r] if own else S.cot.at[k_right, rows_r]
        src_l = g_hbm.at[0, rows_l] if own else S.cot.at[k_left, rows_l]
        return (
            remote(src_r, S.cot.at[k_right, rows_r], S.right_s_sem.at[u], S.right_r_sem.at[u], right),
            remote(src_l, S.cot.at[k_left, rows_l], S.left_s_sem.at[u], S.left_r_sem.at[u], left),
        )

    for u in (0, 1):
        for copy in ring(u, z, z, own=True):
            copy.start()

    def start_w(i, carry):
        load_w((z + i) % 8).start()
        return carry

    lax.fori_loop(1, 8, start_w, 0)

    def sib_columns(k, half):
        copies = []
        for j in (0, 1):
            i = k * 4 + half * 2 + j
            copies.append(
                remote(
                    S.cot.at[k, at256(half), at128(2 * j + 1 - c)],
                    S.cot_sib.at[k, at256(half), pl.ds(j * 128, 128)],
                    S.sib_s_sem.at[i],
                    S.sib_r_sem.at[i],
                    sib,
                )
            )
        return copies

    def y_block(k, half, first=False):
        rows = at256(half)

        for n in range(4):
            cols = pl.ds(n * 256, 256)
            part = mm_nt(S.cot[k, rows, :], S.wv[k, cols, :])
            if first:
                S.y_acc[rows, cols] = part
            else:
                S.y_acc[rows, cols] += part

    def ring_step(t):
        d = t // 2 + 1
        k_right = (z + 8 - d) % 8
        k_left = (z + d) % 8
        for copy in ring(t, k_right, k_left):
            copy.wait_recv()

        @pl.when(t <= 4)
        def _():
            for copy in ring(t + 2, k_right, k_left):
                copy.start()

        for copy in sib_columns(k_right, t % 2) + sib_columns(k_left, 1 - t % 2):
            copy.start()
        y_block(k_right, t % 2)
        y_block(k_left, 1 - t % 2)

    def iota(shape, dim):
        return lax.broadcasted_iota(jnp.int32, shape, dim)

    low_lanes = iota((256, 128), 1) < 64
    lane_row = iota((1, 128), 1)
    lane_masks = [
        jnp.where(lane_row < 64, 1.0, 0.0).astype(BF16),
        jnp.where(lane_row < 64, 0.0, 1.0).astype(BF16),
    ]
    lower = iota((128, 128), 0) >= iota((128, 128), 1)
    upper = iota((128, 128), 1) >= iota((128, 128), 0)

    S.dv[16:, :] = jnp.zeros((112, 512), F32)
    loads[0].wait()
    tril = jnp.where(iota((256, 256), 0) >= iota((256, 256), 1), 1.0, 0.0).astype(BF16)
    for sp in (0, 1):
        rows = pl.ds(sp * 256, 256)
        parts = split3(S.dv[:, rows])
        running = sum(mm_nt(tril, p) for p in parts)
        for h in range(16):
            S.la[h, rows, :] = jnp.broadcast_to(running[:, h : h + 1], (256, 128))
        turned = sum(mm_nt(p[:16], tril) for p in parts)
        for h in range(16):
            S.la_row[sp * 16 + h] = jnp.broadcast_to(turned[h : h + 1, :], (8, 256))

    def pair_log(rows, hp):
        return jnp.where(low_lanes, S.la[2 * hp, rows, :], S.la[2 * hp + 1, rows, :])

    def where_of(it):
        sp = it // 8
        hp = it % 8
        return sp, hp, at256(sp), at128(hp), hp // 4, at128(hp % 4)

    for load in loads[1:4]:
        load.wait()
    for sp in (0, 1):
        rows = pl.ds(sp * 256, 256)
        S.b_t[sp] = S.bv[rows, :].astype(F32).T.astype(BF16)
        S.c_t[sp] = S.cv[rows, :].astype(F32).T.astype(BF16)

    def span_add(it, carry):
        sp, hp, rows, lanes, half, half_lanes = where_of(it)
        logs = pair_log(rows, hp)
        total = logs[255:256, :]
        S.tots[sp, half, :, half_lanes] = jnp.broadcast_to(total, (8, 128))
        scaled = (jnp.exp(total - logs) * S.xv[rows, lanes].astype(F32)).astype(BF16)
        S.x_end[rows, lanes] = scaled
        S.adds[sp, half, :, half_lanes] = mm(S.b_t[sp], scaled)
        return carry

    lax.fori_loop(0, 16, span_add, 0, unroll=8)

    def row(ref):
        return ref[0:1, :]

    def exchange_1(way):
        for half in (0, 1):
            S.l1_out[way, half] = S.loc[way, half].astype(BF16)
        l1_copy(way).start()

    def l1_copy(way):
        return remote(
            S.l1_out.at[way, 1 - c], S.l1_in.at[way], S.l1_s_sem.at[way], S.l1_r_sem.at[way], sib
        )

    def l2_copy(way, dist):
        to = x + dist if way == 0 else x - dist
        i = way * 3 + dist - 1
        return remote(
            S.l2_out.at[way],
            S.l2_in.at[way, dist - 1],
            S.l2_s_sem.at[i],
            S.l2_r_sem.at[i],
            x_peer(to),
        )

    def l3_copy(way):
        return remote(S.l3_out.at[way], S.l3_in.at[way], S.l3_s_sem.at[way], S.l3_r_sem.at[way], sib)

    def place_of(way):
        return (c, x) if way == 0 else (1 - c, 3 - x)

    def exchange_2(way):
        core, chip = place_of(way)
        l1_copy(way).wait_recv()
        one = jnp.ones((1, 512), F32)
        a = jnp.where(core == 0, jnp.exp(row(S.d_sib)), one)
        b = jnp.where(core == 0, one, jnp.exp(S.d_own[c, 0:1, :]))
        S.l2_out[way] = (a * S.loc[way, c] + b * S.l1_in[way].astype(F32)).astype(BF16)
        for dist in (1, 2, 3):

            @pl.when(chip + dist <= 3)
            def _():
                l2_copy(way, dist).start()

    def exchange_3(way):
        core, chip = place_of(way)
        S.inh[...] = jnp.zeros_like(S.inh)
        near = 3 if way == 0 else 1
        for dist in (1, 2, 3):

            @pl.when(chip >= dist)
            def _():
                l2_copy(way, dist).wait_recv()
                term = S.l2_in[way, dist - 1].astype(F32)
                if dist == 2:
                    term = term * jnp.exp(S.d_chip[near, 0:1, :])
                if dist == 3:
                    term = term * jnp.exp(S.d_chip[near, 0:1, :] + S.d_chip[2, 0:1, :])
                S.inh[...] += term

        into = S.inh[...]
        own = S.loc[way, c] + jnp.exp(S.d_own[c, 0:1, :]) * into
        S.l3_out[way] = jnp.where(core == 0, own, into).astype(BF16)
        l3_copy(way).start()
        other = S.l1_in[way].astype(F32) + jnp.exp(row(S.d_sib)) * into
        S.inc[way, c] = jnp.where(core == 0, into, other)

    def exchange_4(way):
        l3_copy(way).wait_recv()
        S.inc[way, 1 - c] = S.l3_in[way].astype(F32)

    def d_sib_copy():
        return remote(S.d_own.at[1 - c], S.d_sib, S.ds_s_sem.at[0], S.ds_r_sem.at[0], sib)

    def d_chip_copy(dist):
        return remote(
            S.d_chip.at[0],
            S.d_chip.at[4 - dist],
            S.dc_s_sem.at[dist],
            S.dc_r_sem.at[4 - dist],
            x_peer((x + dist) % 4),
        )

    for half in (0, 1):
        S.d_own[half] = S.tots[0, half] + S.tots[1, half]
        S.loc[0, half] = jnp.exp(S.tots[1, half, 0:1, :]) * S.adds[0, half] + S.adds[1, half]
    d_sib_copy().start()
    exchange_1(0)

    loads[4].wait()
    for half in (0, 1):
        for copy in sib_columns(z, half):
            copy.start()
    load_w(z).wait()
    for half in (0, 1):
        y_block(z, half, first=True)

    d_sib_copy().wait_recv()
    S.d_chip[0] = S.d_own[c] + S.d_sib[...]
    for dist in (1, 2, 3):
        d_chip_copy(dist).start()
    exchange_2(0)

    for sp in (0, 1):
        rows = pl.ds(sp * 256, 256)
        S.aff[sp] = mm_nt(S.cv[rows, :], S.bv[rows, :])
        S.aff_t[sp] = mm_nt(S.bv[rows, :], S.cv[rows, :])

    def within_span(it, carry):
        sp, hp, rows, lanes, half, half_lanes = where_of(it)
        values = S.xv[rows, lanes]
        top = jnp.zeros((128, 128), F32)
        bottom = jnp.zeros((128, 128), F32)
        for u in (0, 1):
            col = S.la[2 * hp + u, rows, :]
            line = S.la_row[sp * 16 + 2 * hp + u, 0:1, :]
            tl = jnp.exp(jnp.where(lower, col[:128] - line[:, :128], NEG)) * S.aff[sp, :128, :128]
            bl = jnp.exp(col[128:] - line[:, :128]) * S.aff[sp, 128:, :128]
            br = jnp.exp(jnp.where(lower, col[128:] - line[:, 128:], NEG)) * S.aff[sp, 128:, 128:]
            mine = values * lane_masks[u]
            top += mm(tl.astype(BF16), mine[:128])
            bottom += mm(jnp.concatenate([bl.astype(BF16), br.astype(BF16)], axis=1), mine)
        S.inner[at256(sp, 128), lanes] = top
        S.inner[at128(2 * sp + 1), lanes] = bottom
        return carry

    lax.fori_loop(0, 16, within_span, 0, unroll=8)

    lax.fori_loop(1, 8, lambda i, carry: (load_w((z + i) % 8).wait(), carry)[1], 0)
    for dist in (1, 2, 3):
        d_chip_copy(dist).wait_recv()
    ring_step(0)

    exchange_3(0)
    ring_step(1)
    exchange_4(0)
    for half in (0, 1):
        S.ent[0, half] = S.inc[0, half].astype(BF16)
        S.ent[1, half] = (
            jnp.exp(S.tots[0, half, 0:1, :]) * S.inc[0, half] + S.adds[0, half]
        ).astype(BF16)

    def scan_rows(it, carry):
        sp, hp, rows, lanes, half, half_lanes = where_of(it)
        carried = mm(S.cv[rows, :], S.ent[sp, half, :, half_lanes])
        value = S.inner[rows, lanes] + jnp.exp(pair_log(rows, hp)) * carried
        S.scan_t[lanes, rows] = value.T.astype(BF16)
        return carry

    lax.fori_loop(0, 16, scan_rows, 0, unroll=8)
    scan_copy = remote(S.scan_t, S.scan_t_sib, S.scan_s_sem.at[0], S.scan_r_sem.at[0], sib)
    scan_copy.start()

    def block_of(b):
        d = (b + 1) // 2
        return (z + jnp.where(b % 2 == 1, 8 - d, d)) % 8

    def xa_copy(k, j):
        to = 2 * (k % 2) + j
        slot = (x + 4 - to) % 4 - 1
        return to, remote(
            S.part.at[k, pl.ds(0, X_ROWS), pl.ds(j * 128, 128)],
            S.xa_in.at[k // 2, slot],
            S.xa_s_sem.at[k * 2 + j],
            S.xa_r_sem.at[(k // 2) * 3 + slot],
            x_peer(to),
        )

    def ya_copy(k):
        to = k // 2
        slot = (y + 4 - to) % 4 - 1
        return to, remote(
            S.part.at[k, pl.ds(X_ROWS, Y_ROWS)],
            S.ya_in.at[k % 2, slot],
            S.ya_s_sem.at[k],
            S.ya_r_sem.at[(k % 2) * 3 + slot],
            y_peer(to),
        )

    def xb_copy(k):
        to = k // 2
        slot = (y + 4 - to) % 4 - 1
        return to, remote(
            S.xq.at[to], S.xb_in.at[slot], S.xb_s_sem.at[to], S.xb_r_sem.at[slot], y_peer(to)
        )

    def yb_copy(k, j):
        to = 2 * (k % 2) + j
        slot = (x + 4 - to) % 4 - 1
        return to, remote(
            S.yq.at[k % 2, :, pl.ds(j * 128, 128)],
            S.yb_in.at[slot],
            S.yb_s_sem.at[to],
            S.yb_r_sem.at[slot],
            x_peer(to),
        )

    def weight_part(b, carry):
        k = block_of(b)
        for half in (0, 1):
            for copy in sib_columns(k, half):
                copy.wait_recv()

        for m in range(4):
            rows = pl.ds(m * 256, 256)
            mine = jnp.concatenate(
                [S.cot[k, :, at128(c)], S.cot[k, :, at128(2 + c)]], axis=1
            )
            total = mm(S.scan_t[rows, :], mine) + mm(S.scan_t_sib[rows, :], S.cot_sib[k])
            S.part[k, rows, :] = total.astype(BF16)
        for j in (0, 1):
            to, copy = xa_copy(k, j)
            pl.when(to != x)(copy.start)
        to, copy = ya_copy(k)
        pl.when(to != y)(copy.start)
        return carry

    def wait_in(buffer, sem):
        remote(buffer, buffer, sem, sem, sib).wait_recv()

    def weight_turn(b, carry):
        k = block_of(b)
        yk = k // 2
        kx = k % 2

        @pl.when(x // 2 == kx)
        def _():
            for i in (0, 1, 2):
                wait_in(S.xa_in.at[yk, i], S.xa_r_sem.at[yk * 3 + i])
            total = S.part[k, pl.ds(0, X_ROWS), at128(x % 2)].astype(F32)
            for i in (0, 1, 2):
                total = total + S.xa_in[yk, i].astype(F32)
            S.xq[yk] = total.astype(BF16)
            to, copy = xb_copy(k)
            pl.when(to != y)(copy.start)

        @pl.when(yk == y)
        def _():
            for i in (0, 1, 2):
                wait_in(S.ya_in.at[kx, i], S.ya_r_sem.at[kx * 3 + i])
            for j in (0, 1):
                cols = pl.ds(j * 128, 128)
                total = S.part[k, pl.ds(X_ROWS, Y_ROWS), cols].astype(F32)
                for i in (0, 1, 2):
                    total = total + S.ya_in[kx, i, :, cols].astype(F32)
                S.yq[kx, :, cols] = total.astype(BF16)
                to, copy = yb_copy(k, j)
                pl.when(to != x)(copy.start)

        return carry

    def turned_weights(it, carry):
        sp, hp, rows, lanes, half, half_lanes = where_of(it)
        for u in (0, 1):
            i = sp * 16 + 2 * hp + u
            col = S.la[2 * hp + u, rows, :]
            line = S.la_row[i, 0:1, :]
            tl = jnp.exp(jnp.where(upper, line[:, :128] - col[:128], NEG))
            tr = jnp.exp(line[:, 128:] - col[:128])
            br = jnp.exp(jnp.where(upper, line[:, 128:] - col[128:], NEG))
            S.within_t[i, 0] = tl.astype(BF16)
            S.within_t[i, 1] = tr.astype(BF16)
            S.within_t[i, 2] = br.astype(BF16)
            S.weights_t[i, 0] = (tl * S.aff_t[sp, :128, :128]).astype(BF16)
            S.weights_t[i, 1] = (tr * S.aff_t[sp, :128, 128:]).astype(BF16)
            S.weights_t[i, 2] = (br * S.aff_t[sp, 128:, 128:]).astype(BF16)
        return carry

    scan_copy.wait_recv()

    def ring_pair(i, carry):
        pl.when(i > 0)(lambda: ring_step(2 * i + 1))
        lax.fori_loop(jnp.where(i == 0, 0, 2 * i + 1), 2 * i + 3, weight_part, 0)
        lax.fori_loop(6 * i, jnp.minimum(6 * i + 6, 16), turned_weights, 0)
        lax.fori_loop(1, jnp.where(i == 2, 3, 1), weight_turn, 0)
        ring_step(2 * i + 2)
        lax.fori_loop(0, jnp.where(i == 1, 1, 0), weight_turn, 0)
        return carry

    lax.fori_loop(0, 3, ring_pair, 0)

    def pull(it, carry):
        sp, hp, rows, lanes, half, half_lanes = where_of(it)
        grad = S.y_acc[rows, lanes].astype(BF16)
        S.gy[rows, lanes] = grad
        scaled = (jnp.exp(pair_log(rows, hp)) * grad.astype(F32)).astype(BF16)
        S.gy_start[rows, lanes] = scaled
        S.adds[sp, half, :, half_lanes] = mm(S.c_t[sp], scaled)
        return carry

    lax.fori_loop(0, 16, pull, 0, unroll=8)
    for half in (0, 1):
        S.loc[1, half] = S.adds[0, half] + jnp.exp(S.tots[0, half, 0:1, :]) * S.adds[1, half]
    exchange_1(1)
    weight_part(7, 0)
    exchange_2(1)
    lax.fori_loop(3, 5, weight_turn, 0)

    def within_back(it, carry):
        sp, hp, rows, lanes, half, half_lanes = where_of(it)
        values = S.xv[rows, lanes]
        grads = S.gy[rows, lanes]
        top = jnp.zeros((128, 128), F32)
        bottom = jnp.zeros((128, 128), F32)
        tl = jnp.zeros((128, 128), F32)
        tr = jnp.zeros((128, 128), F32)
        br = jnp.zeros((128, 128), F32)
        for u in (0, 1):
            i = sp * 16 + 2 * hp + u
            mine = values * lane_masks[u]
            grad = grads * lane_masks[u]
            pair_top = mm_nt(mine[:128], grads)
            pair_bottom = mm_nt(mine[128:], grads[128:])
            tl += pair_top[:, :128] * S.within_t[i, 0].astype(F32)
            tr += pair_top[:, 128:] * S.within_t[i, 1].astype(F32)
            br += pair_bottom * S.within_t[i, 2].astype(F32)
            top += mm(jnp.concatenate([S.weights_t[i, 0], S.weights_t[i, 1]], axis=1), grad)
            bottom += mm(S.weights_t[i, 2], grad[128:])
        S.inner[at256(sp, 128), lanes] = top
        S.inner[at128(2 * sp + 1), lanes] = bottom
        S.aff_grad[sp, :128, :128] += tl
        S.aff_grad[sp, :128, 128:] += tr
        S.aff_grad[sp, 128:, 128:] += br
        return carry

    S.aff_grad[...] = jnp.zeros_like(S.aff_grad)
    lax.fori_loop(0, 16, within_back, 0, unroll=8)

    for sp in (0, 1):
        rows = pl.ds(sp * 256, 256)
        grad = mm_nt(S.gy_start[rows, :512], S.ent[sp, 0]) + mm_nt(S.gy_start[rows, 512:], S.ent[sp, 1])
        tl = S.aff_grad[sp, :128, :128].T.astype(BF16)
        tr = S.aff_grad[sp, :128, 128:].T.astype(BF16)
        br = S.aff_grad[sp, 128:, 128:].T.astype(BF16)
        writes = S.bv[rows, :]
        S.c_out[pl.ds(sp * 256, 128), :] = (grad[:128] + mm(tl, writes[:128])).astype(BF16)
        S.c_out[pl.ds(sp * 256 + 128, 128), :] = (
            grad[128:] + mm(jnp.concatenate([tr, br], axis=1), writes)
        ).astype(BF16)
    store_c = pltpu.make_async_copy(S.c_out, cg_hbm.at[0], S.store_sem.at[0])
    store_c.start()

    lax.fori_loop(5, 7, weight_turn, 0)
    exchange_3(1)
    weight_turn(7, 0)
    exchange_4(1)
    for half in (0, 1):
        S.lv[1, half] = S.inc[1, half].astype(BF16)
        S.lv[0, half] = (
            S.adds[1, half] + jnp.exp(S.tots[1, half, 0:1, :]) * S.inc[1, half]
        ).astype(BF16)

    def x_final(it, carry):
        sp, hp, rows, lanes, half, half_lanes = where_of(it)
        logs = pair_log(rows, hp)
        to_end = jnp.exp(logs[255:256, :] - logs)
        late = mm(S.bv[rows, :], S.lv[sp, half, :, half_lanes])
        S.x_out[rows, lanes] = (S.inner[rows, lanes] + to_end * late).astype(BF16)
        return carry

    lax.fori_loop(0, 16, x_final, 0, unroll=8)
    store_x = pltpu.make_async_copy(S.x_out, xg_hbm.at[0], S.store_sem.at[1])
    store_x.start()

    for sp in (0, 1):
        rows = pl.ds(sp * 256, 256)
        grad = mm_nt(S.x_end[rows, :512], S.lv[sp, 0]) + mm_nt(S.x_end[rows, 512:], S.lv[sp, 1])
        top = S.aff_grad[sp, :128, :].astype(BF16)
        br = S.aff_grad[sp, 128:, 128:].astype(BF16)
        reads = S.cv[rows, :]
        S.b_out[pl.ds(sp * 256, 128), :] = (grad[:128] + mm(top, reads)).astype(BF16)
        S.b_out[pl.ds(sp * 256 + 128, 128), :] = (grad[128:] + mm(br, reads[128:])).astype(BF16)
    store_b = pltpu.make_async_copy(S.b_out, bg_hbm.at[0], S.store_sem.at[2])
    store_b.start()

    for i in (0, 1, 2):
        wait_in(S.xb_in.at[i], S.xb_r_sem.at[i])
    total = S.xq[y].astype(F32)
    for i in (0, 1, 2):
        total = total + S.xb_in[i].astype(F32)
    S.w_out[pl.ds(0, X_ROWS), :] = total.astype(BF16)
    for i in (0, 1, 2):
        wait_in(S.yb_in.at[i], S.yb_r_sem.at[i])
    total = S.yq[x // 2, :, at128(x % 2)].astype(F32)
    for i in (0, 1, 2):
        total = total + S.yb_in[i].astype(F32)
    S.w_out[pl.ds(X_ROWS, Y_ROWS), :] = total.astype(BF16)
    store_w = pltpu.make_async_copy(S.w_out, wg_hbm, S.store_sem.at[3])
    store_w.start()

    def ring_sent(u, carry):
        for copy in ring(u, z, z):
            copy.wait_send()
        return carry

    lax.fori_loop(0, 7, ring_sent, 0)

    def block_sent(k, carry):
        for half in (0, 1):
            for copy in sib_columns(k, half):
                copy.wait_send()
        for j in (0, 1):
            to, copy = xa_copy(k, j)
            pl.when(to != x)(copy.wait_send)
        to, copy = ya_copy(k)
        pl.when(to != y)(copy.wait_send)

        @pl.when(x // 2 == k % 2)
        def _():
            to, copy = xb_copy(k)
            pl.when(to != y)(copy.wait_send)

        @pl.when(k // 2 == y)
        def _():
            for j in (0, 1):
                to, copy = yb_copy(k, j)
                pl.when(to != x)(copy.wait_send)

        return carry

    lax.fori_loop(0, 8, block_sent, 0)
    scan_copy.wait_send()
    d_sib_copy().wait_send()
    for dist in (1, 2, 3):
        d_chip_copy(dist).wait_send()
    for way in (0, 1):
        l1_copy(way).wait_send()
        l3_copy(way).wait_send()
        core, chip = place_of(way)
        for dist in (1, 2, 3):

            @pl.when(chip + dist <= 3)
            def _():
                l2_copy(way, dist).wait_send()

    for store in (store_c, store_x, store_b, store_w):
        store.wait()


def copy_kernel(*refs):
    ins, outs, held, sems = refs[:4], refs[4:8], refs[8:12], refs[12]
    pieces = []
    for n, (src, dst, mid) in enumerate(zip(ins, outs, held)):
        size = 256 if n else 512
        for i in range(1024 // size if n == 0 else 512 // size):
            rows = pl.ds(i * size, size)
            at = (rows,) if n == 0 else (0, rows)
            j = 2 * len(pieces)
            pieces.append(
                (
                    pltpu.make_async_copy(src.at[at], mid.at[at], sems.at[j]),
                    pltpu.make_async_copy(mid.at[at], dst.at[at], sems.at[j + 1]),
                )
            )
    for come, _ in pieces:
        come.start()
    for come, go in pieces:
        come.wait()
        go.start()
    for _, go in pieces:
        go.wait()


def per_device(x_in, b_in, c_in, log_decay, out_weight, out_grad):
    out_shape = (
        jax.ShapeDtypeStruct((1024, 128), BF16),
        jax.ShapeDtypeStruct((1, 512, 1024), BF16),
        jax.ShapeDtypeStruct((1, 512, 128), BF16),
        jax.ShapeDtypeStruct((1, 512, 128), BF16),
    )
    scratch = [pltpu.VMEM(shape, dtype) for shape, dtype in VMEM_SCRATCH.values()]
    scratch += [pltpu.SemaphoreType.DMA(shape) for shape in SEMAPHORES.values()]
    results = pl.pallas_call(
        kernel,
        out_shape=out_shape,
        in_specs=[pl.BlockSpec(memory_space=pl.ANY)] * 6,
        out_specs=[pl.BlockSpec(memory_space=pl.ANY)] * 4,
        scratch_shapes=scratch,
        compiler_params=pltpu.CompilerParams(
            collective_id=0, has_side_effects=True, vmem_limit_bytes=63 * 2**20
        ),
    )(x_in, b_in, c_in, jnp.transpose(log_decay, (0, 2, 1)), out_weight, out_grad)
    return pl.pallas_call(
        copy_kernel,
        out_shape=out_shape,
        in_specs=[pl.BlockSpec(memory_space=pl.ANY)] * 4,
        out_specs=[pl.BlockSpec(memory_space=pl.ANY)] * 4,
        scratch_shapes=[pltpu.VMEM(o.shape, o.dtype) for o in out_shape]
        + [pltpu.SemaphoreType.DMA((16,))],
    )(*results)


def solution(mesh):
    in_specs = (
        P("dp", "seq", "tensor"),
        P("dp", "seq", "tensor"),
        P("dp", "seq", "tensor"),
        P("dp", "seq", "tensor"),
        P("tensor", None),
        P("dp", "seq", "tensor"),
    )
    out_specs = (
        P("tensor", ("dp", "seq")),
        P("dp", "seq", "tensor"),
        P("dp", "seq", "tensor"),
        P("dp", "seq", "tensor"),
    )
    return jax.shard_map(
        per_device, mesh=mesh, in_specs=in_specs, out_specs=out_specs, check_vma=False
    )
```

```python
from types import SimpleNamespace

import jax
import jax.numpy as jnp
from jax import lax
from jax.experimental import pallas as pl
from jax.experimental.pallas import tpu as pltpu
from jax.sharding import PartitionSpec as P

F32 = jnp.float32
BF16 = jnp.bfloat16
MESH = pl.DeviceIdType.MESH
NEG = -1e30
X_ROWS = 608
Y_ROWS = 1024 - X_ROWS

VMEM_SCRATCH = dict(
    xv=((512, 1024), BF16),
    bv=((512, 128), BF16),
    cv=((512, 128), BF16),
    dv=((128, 512), F32),
    wv=((8, 1024, 512), BF16),
    cot=((8, 512, 512), BF16),
    cot_sib=((8, 512, 256), BF16),
    b_t=((2, 128, 256), BF16),
    c_t=((2, 128, 256), BF16),
    la=((16, 512, 128), F32),
    la_row=((32, 8, 256), F32),
    tots=((2, 2, 8, 512), F32),
    aff=((2, 256, 256), F32),
    aff_t=((2, 256, 256), F32),
    within_t=((32, 3, 128, 128), BF16),
    weights_t=((32, 3, 128, 128), BF16),
    x_end=((512, 1024), BF16),
    inner=((512, 1024), F32),
    y_acc=((512, 1024), F32),
    gy=((512, 1024), BF16),
    gy_start=((512, 1024), BF16),
    scan_t=((1024, 512), BF16),
    scan_t_sib=((1024, 512), BF16),
    adds=((2, 2, 128, 512), F32),
    loc=((2, 2, 128, 512), F32),
    inc=((2, 2, 128, 512), F32),
    inh=((128, 512), F32),
    ent=((2, 2, 128, 512), BF16),
    lv=((2, 2, 128, 512), BF16),
    l1_out=((2, 2, 128, 512), BF16),
    l1_in=((2, 128, 512), BF16),
    l2_out=((2, 128, 512), BF16),
    l2_in=((2, 3, 128, 512), BF16),
    l3_out=((2, 128, 512), BF16),
    l3_in=((2, 128, 512), BF16),
    d_own=((2, 8, 512), F32),
    d_sib=((8, 512), F32),
    d_chip=((4, 8, 512), F32),
    part=((8, 1024, 256), BF16),
    xa_in=((4, 3, X_ROWS, 128), BF16),
    ya_in=((2, 3, Y_ROWS, 256), BF16),
    xq=((4, X_ROWS, 128), BF16),
    yq=((2, Y_ROWS, 256), BF16),
    xb_in=((3, X_ROWS, 128), BF16),
    yb_in=((3, Y_ROWS, 128), BF16),
    aff_grad=((2, 256, 256), F32),
    x_out=((512, 1024), BF16),
    b_out=((512, 128), BF16),
    c_out=((512, 128), BF16),
    w_out=((1024, 128), BF16),
)
SEMAPHORES = dict(
    load=(6,),
    load_w=(8,),
    right_s=(7,),
    right_r=(7,),
    left_s=(7,),
    left_r=(7,),
    sib_s=(32,),
    sib_r=(32,),
    scan_s=(1,),
    scan_r=(1,),
    ds_s=(1,),
    ds_r=(1,),
    dc_s=(4,),
    dc_r=(4,),
    l1_s=(2,),
    l1_r=(2,),
    l2_s=(6,),
    l2_r=(6,),
    l3_s=(2,),
    l3_r=(2,),
    xa_s=(16,),
    xa_r=(12,),
    ya_s=(8,),
    ya_r=(6,),
    xb_s=(4,),
    xb_r=(3,),
    yb_s=(4,),
    yb_r=(3,),
    store=(4,),
)
NAMES = list(VMEM_SCRATCH) + [f"{n}_sem" for n in SEMAPHORES]


def mm(a, b):
    return jnp.dot(a, b, preferred_element_type=F32)


def mm_nt(a, b):
    return lax.dot_general(a, b, (((1,), (1,)), ((), ())), preferred_element_type=F32)


def at128(i, size=128):
    return pl.ds(pl.multiple_of(i * 128, 128), size)


def at256(i, size=256):
    return pl.ds(pl.multiple_of(i * 256, 256), size)


def split3(v):
    hi = v.astype(BF16)
    rest = v - hi.astype(F32)
    mid = rest.astype(BF16)
    return hi, mid, (rest - mid.astype(F32)).astype(BF16)


def kernel(x_hbm, b_hbm, c_hbm, d_hbm, w_hbm, g_hbm, wg_hbm, xg_hbm, bg_hbm, cg_hbm, *scratch):
    S = SimpleNamespace(**dict(zip(NAMES, scratch)))
    y = lax.axis_index("dp")
    s = lax.axis_index("seq")
    z = lax.axis_index("tensor")
    x = s // 2
    c = s % 2
    sib = (y, x * 2 + (1 - c), z)
    right = (y, s, (z + 1) % 8)
    left = (y, s, (z + 7) % 8)

    def x_peer(xx):
        return (y, xx * 2 + c, z)

    def y_peer(yy):
        return (yy, s, z)

    def remote(src, dst, send_sem, recv_sem, device):
        return pltpu.make_async_remote_copy(
            src_ref=src,
            dst_ref=dst,
            send_sem=send_sem,
            recv_sem=recv_sem,
            device_id=device,
            device_id_type=MESH,
        )

    loads = [
        pltpu.make_async_copy(d_hbm.at[0], S.dv.at[pl.ds(0, 16)], S.load_sem.at[0]),
        pltpu.make_async_copy(b_hbm.at[0], S.bv, S.load_sem.at[1]),
        pltpu.make_async_copy(c_hbm.at[0], S.cv, S.load_sem.at[2]),
        pltpu.make_async_copy(x_hbm.at[0], S.xv, S.load_sem.at[3]),
        pltpu.make_async_copy(g_hbm.at[0], S.cot.at[z], S.load_sem.at[4]),
    ]
    for load in loads:
        load.start()

    def load_w(k):
        return pltpu.make_async_copy(
            w_hbm.at[:, pl.ds(pl.multiple_of(k * 512, 512), 512)], S.wv.at[k], S.load_w_sem.at[k]
        )

    load_w(z).start()

    barrier = pltpu.get_barrier_semaphore()
    peers = [sib, right, left]
    peers += [x_peer((x + i) % 4) for i in (1, 2, 3)] + [y_peer((y + i) % 4) for i in (1, 2, 3)]
    for peer in peers:
        pl.semaphore_signal(barrier, inc=1, device_id=peer, device_id_type=MESH)
    pl.semaphore_wait(barrier, len(peers))

    def ring(u, k_right, k_left, own=False):
        half_r = u % 2
        half_l = 1 - u % 2
        rows_r = at256(half_r)
        rows_l = at256(half_l)
        src_r = g_hbm.at[0, rows_r] if own else S.cot.at[k_right, rows_r]
        src_l = g_hbm.at[0, rows_l] if own else S.cot.at[k_left, rows_l]
        return (
            remote(src_r, S.cot.at[k_right, rows_r], S.right_s_sem.at[u], S.right_r_sem.at[u], right),
            remote(src_l, S.cot.at[k_left, rows_l], S.left_s_sem.at[u], S.left_r_sem.at[u], left),
        )

    for u in (0, 1):
        for copy in ring(u, z, z, own=True):
            copy.start()

    def start_w(i, carry):
        load_w((z + i) % 8).start()
        return carry

    lax.fori_loop(1, 8, start_w, 0)

    def sib_columns(k, half):
        copies = []
        for j in (0, 1):
            i = k * 4 + half * 2 + j
            copies.append(
                remote(
                    S.cot.at[k, at256(half), at128(2 * j + 1 - c)],
                    S.cot_sib.at[k, at256(half), pl.ds(j * 128, 128)],
                    S.sib_s_sem.at[i],
                    S.sib_r_sem.at[i],
                    sib,
                )
            )
        return copies

    def y_block(k, half, first=False):
        rows = at256(half)

        for n in range(4):
            cols = pl.ds(n * 256, 256)
            part = mm_nt(S.cot[k, rows, :], S.wv[k, cols, :])
            if first:
                S.y_acc[rows, cols] = part
            else:
                S.y_acc[rows, cols] += part

    def ring_step(t):
        d = t // 2 + 1
        k_right = (z + 8 - d) % 8
        k_left = (z + d) % 8
        for copy in ring(t, k_right, k_left):
            copy.wait_recv()

        @pl.when(t <= 4)
        def _():
            for copy in ring(t + 2, k_right, k_left):
                copy.start()

        for copy in sib_columns(k_right, t % 2) + sib_columns(k_left, 1 - t % 2):
            copy.start()
        y_block(k_right, t % 2)
        y_block(k_left, 1 - t % 2)

    def iota(shape, dim):
        return lax.broadcasted_iota(jnp.int32, shape, dim)

    low_lanes = iota((256, 128), 1) < 64
    lane_row = iota((1, 128), 1)
    lane_masks = [
        jnp.where(lane_row < 64, 1.0, 0.0).astype(BF16),
        jnp.where(lane_row < 64, 0.0, 1.0).astype(BF16),
    ]
    lower = iota((128, 128), 0) >= iota((128, 128), 1)
    upper = iota((128, 128), 1) >= iota((128, 128), 0)

    S.dv[16:, :] = jnp.zeros((112, 512), F32)
    loads[0].wait()
    tril = jnp.where(iota((256, 256), 0) >= iota((256, 256), 1), 1.0, 0.0).astype(BF16)
    for sp in (0, 1):
        rows = pl.ds(sp * 256, 256)
        parts = split3(S.dv[:, rows])
        running = sum(mm_nt(tril, p) for p in parts)
        for h in range(16):
            S.la[h, rows, :] = jnp.broadcast_to(running[:, h : h + 1], (256, 128))
        turned = sum(mm_nt(p[:16], tril) for p in parts)
        for h in range(16):
            S.la_row[sp * 16 + h] = jnp.broadcast_to(turned[h : h + 1, :], (8, 256))

    def pair_log(rows, hp):
        return jnp.where(low_lanes, S.la[2 * hp, rows, :], S.la[2 * hp + 1, rows, :])

    def where_of(it):
        sp = it // 8
        hp = it % 8
        return sp, hp, at256(sp), at128(hp), hp // 4, at128(hp % 4)

    for load in loads[1:4]:
        load.wait()
    for sp in (0, 1):
        rows = pl.ds(sp * 256, 256)
        S.b_t[sp] = S.bv[rows, :].astype(F32).T.astype(BF16)
        S.c_t[sp] = S.cv[rows, :].astype(F32).T.astype(BF16)

    def span_add(it, carry):
        sp, hp, rows, lanes, half, half_lanes = where_of(it)
        logs = pair_log(rows, hp)
        total = logs[255:256, :]
        S.tots[sp, half, :, half_lanes] = jnp.broadcast_to(total, (8, 128))
        scaled = (jnp.exp(total - logs) * S.xv[rows, lanes].astype(F32)).astype(BF16)
        S.x_end[rows, lanes] = scaled
        S.adds[sp, half, :, half_lanes] = mm(S.b_t[sp], scaled)
        return carry

    lax.fori_loop(0, 16, span_add, 0, unroll=8)

    def row(ref):
        return ref[0:1, :]

    def exchange_1(way):
        for half in (0, 1):
            S.l1_out[way, half] = S.loc[way, half].astype(BF16)
        l1_copy(way).start()

    def l1_copy(way):
        return remote(
            S.l1_out.at[way, 1 - c], S.l1_in.at[way], S.l1_s_sem.at[way], S.l1_r_sem.at[way], sib
        )

    def l2_copy(way, dist):
        to = x + dist if way == 0 else x - dist
        i = way * 3 + dist - 1
        return remote(
            S.l2_out.at[way],
            S.l2_in.at[way, dist - 1],
            S.l2_s_sem.at[i],
            S.l2_r_sem.at[i],
            x_peer(to),
        )

    def l3_copy(way):
        return remote(S.l3_out.at[way], S.l3_in.at[way], S.l3_s_sem.at[way], S.l3_r_sem.at[way], sib)

    def place_of(way):
        return (c, x) if way == 0 else (1 - c, 3 - x)

    def exchange_2(way):
        core, chip = place_of(way)
        l1_copy(way).wait_recv()
        one = jnp.ones((1, 512), F32)
        a = jnp.where(core == 0, jnp.exp(row(S.d_sib)), one)
        b = jnp.where(core == 0, one, jnp.exp(S.d_own[c, 0:1, :]))
        S.l2_out[way] = (a * S.loc[way, c] + b * S.l1_in[way].astype(F32)).astype(BF16)
        for dist in (1, 2, 3):

            @pl.when(chip + dist <= 3)
            def _():
                l2_copy(way, dist).start()

    def exchange_3(way):
        core, chip = place_of(way)
        S.inh[...] = jnp.zeros_like(S.inh)
        near = 3 if way == 0 else 1
        for dist in (1, 2, 3):

            @pl.when(chip >= dist)
            def _():
                l2_copy(way, dist).wait_recv()
                term = S.l2_in[way, dist - 1].astype(F32)
                if dist == 2:
                    term = term * jnp.exp(S.d_chip[near, 0:1, :])
                if dist == 3:
                    term = term * jnp.exp(S.d_chip[near, 0:1, :] + S.d_chip[2, 0:1, :])
                S.inh[...] += term

        into = S.inh[...]
        own = S.loc[way, c] + jnp.exp(S.d_own[c, 0:1, :]) * into
        S.l3_out[way] = jnp.where(core == 0, own, into).astype(BF16)
        l3_copy(way).start()
        other = S.l1_in[way].astype(F32) + jnp.exp(row(S.d_sib)) * into
        S.inc[way, c] = jnp.where(core == 0, into, other)

    def exchange_4(way):
        l3_copy(way).wait_recv()
        S.inc[way, 1 - c] = S.l3_in[way].astype(F32)

    def d_sib_copy():
        return remote(S.d_own.at[1 - c], S.d_sib, S.ds_s_sem.at[0], S.ds_r_sem.at[0], sib)

    def d_chip_copy(dist):
        return remote(
            S.d_chip.at[0],
            S.d_chip.at[4 - dist],
            S.dc_s_sem.at[dist],
            S.dc_r_sem.at[4 - dist],
            x_peer((x + dist) % 4),
        )

    for half in (0, 1):
        S.d_own[half] = S.tots[0, half] + S.tots[1, half]
        S.loc[0, half] = jnp.exp(S.tots[1, half, 0:1, :]) * S.adds[0, half] + S.adds[1, half]
    d_sib_copy().start()
    exchange_1(0)

    loads[4].wait()
    for half in (0, 1):
        for copy in sib_columns(z, half):
            copy.start()
    load_w(z).wait()
    for half in (0, 1):
        y_block(z, half, first=True)

    d_sib_copy().wait_recv()
    S.d_chip[0] = S.d_own[c] + S.d_sib[...]
    for dist in (1, 2, 3):
        d_chip_copy(dist).start()
    exchange_2(0)

    for sp in (0, 1):
        rows = pl.ds(sp * 256, 256)
        S.aff[sp] = mm_nt(S.cv[rows, :], S.bv[rows, :])
        S.aff_t[sp] = mm_nt(S.bv[rows, :], S.cv[rows, :])

    def within_span(it, carry):
        sp, hp, rows, lanes, half, half_lanes = where_of(it)
        values = S.xv[rows, lanes]
        top = jnp.zeros((128, 128), F32)
        bottom = jnp.zeros((128, 128), F32)
        for u in (0, 1):
            col = S.la[2 * hp + u, rows, :]
            line = S.la_row[sp * 16 + 2 * hp + u, 0:1, :]
            tl = jnp.exp(jnp.where(lower, col[:128] - line[:, :128], NEG)) * S.aff[sp, :128, :128]
            bl = jnp.exp(col[128:] - line[:, :128]) * S.aff[sp, 128:, :128]
            br = jnp.exp(jnp.where(lower, col[128:] - line[:, 128:], NEG)) * S.aff[sp, 128:, 128:]
            mine = values * lane_masks[u]
            top += mm(tl.astype(BF16), mine[:128])
            bottom += mm(jnp.concatenate([bl.astype(BF16), br.astype(BF16)], axis=1), mine)
        S.inner[at256(sp, 128), lanes] = top
        S.inner[at128(2 * sp + 1), lanes] = bottom
        return carry

    lax.fori_loop(0, 16, within_span, 0, unroll=8)

    lax.fori_loop(1, 8, lambda i, carry: (load_w((z + i) % 8).wait(), carry)[1], 0)
    for dist in (1, 2, 3):
        d_chip_copy(dist).wait_recv()
    ring_step(0)

    exchange_3(0)
    ring_step(1)
    exchange_4(0)
    for half in (0, 1):
        S.ent[0, half] = S.inc[0, half].astype(BF16)
        S.ent[1, half] = (
            jnp.exp(S.tots[0, half, 0:1, :]) * S.inc[0, half] + S.adds[0, half]
        ).astype(BF16)

    def scan_rows(it, carry):
        sp, hp, rows, lanes, half, half_lanes = where_of(it)
        carried = mm(S.cv[rows, :], S.ent[sp, half, :, half_lanes])
        value = S.inner[rows, lanes] + jnp.exp(pair_log(rows, hp)) * carried
        S.scan_t[lanes, rows] = value.T.astype(BF16)
        return carry

    lax.fori_loop(0, 16, scan_rows, 0, unroll=8)
    scan_copy = remote(S.scan_t, S.scan_t_sib, S.scan_s_sem.at[0], S.scan_r_sem.at[0], sib)
    scan_copy.start()

    def block_of(b):
        d = (b + 1) // 2
        return (z + jnp.where(b % 2 == 1, 8 - d, d)) % 8

    def xa_copy(k, j):
        to = 2 * (k % 2) + j
        slot = (x + 4 - to) % 4 - 1
        return to, remote(
            S.part.at[k, pl.ds(0, X_ROWS), pl.ds(j * 128, 128)],
            S.xa_in.at[k // 2, slot],
            S.xa_s_sem.at[k * 2 + j],
            S.xa_r_sem.at[(k // 2) * 3 + slot],
            x_peer(to),
        )

    def ya_copy(k):
        to = k // 2
        slot = (y + 4 - to) % 4 - 1
        return to, remote(
            S.part.at[k, pl.ds(X_ROWS, Y_ROWS)],
            S.ya_in.at[k % 2, slot],
            S.ya_s_sem.at[k],
            S.ya_r_sem.at[(k % 2) * 3 + slot],
            y_peer(to),
        )

    def xb_copy(k):
        to = k // 2
        slot = (y + 4 - to) % 4 - 1
        return to, remote(
            S.xq.at[to], S.xb_in.at[slot], S.xb_s_sem.at[to], S.xb_r_sem.at[slot], y_peer(to)
        )

    def yb_copy(k, j):
        to = 2 * (k % 2) + j
        slot = (x + 4 - to) % 4 - 1
        return to, remote(
            S.yq.at[k % 2, :, pl.ds(j * 128, 128)],
            S.yb_in.at[slot],
            S.yb_s_sem.at[to],
            S.yb_r_sem.at[slot],
            x_peer(to),
        )

    def weight_part(b, carry):
        k = block_of(b)
        for half in (0, 1):
            for copy in sib_columns(k, half):
                copy.wait_recv()

        for m in range(4):
            rows = pl.ds(m * 256, 256)
            mine = jnp.concatenate(
                [S.cot[k, :, at128(c)], S.cot[k, :, at128(2 + c)]], axis=1
            )
            total = mm(S.scan_t[rows, :], mine) + mm(S.scan_t_sib[rows, :], S.cot_sib[k])
            S.part[k, rows, :] = total.astype(BF16)
        for j in (0, 1):
            to, copy = xa_copy(k, j)
            pl.when(to != x)(copy.start)
        to, copy = ya_copy(k)
        pl.when(to != y)(copy.start)
        return carry

    def wait_in(buffer, sem):
        remote(buffer, buffer, sem, sem, sib).wait_recv()

    def weight_turn(b, carry):
        k = block_of(b)
        yk = k // 2
        kx = k % 2

        @pl.when(x // 2 == kx)
        def _():
            for i in (0, 1, 2):
                wait_in(S.xa_in.at[yk, i], S.xa_r_sem.at[yk * 3 + i])
            total = S.part[k, pl.ds(0, X_ROWS), at128(x % 2)].astype(F32)
            for i in (0, 1, 2):
                total = total + S.xa_in[yk, i].astype(F32)
            S.xq[yk] = total.astype(BF16)
            to, copy = xb_copy(k)
            pl.when(to != y)(copy.start)

        @pl.when(yk == y)
        def _():
            for i in (0, 1, 2):
                wait_in(S.ya_in.at[kx, i], S.ya_r_sem.at[kx * 3 + i])
            for j in (0, 1):
                cols = pl.ds(j * 128, 128)
                total = S.part[k, pl.ds(X_ROWS, Y_ROWS), cols].astype(F32)
                for i in (0, 1, 2):
                    total = total + S.ya_in[kx, i, :, cols].astype(F32)
                S.yq[kx, :, cols] = total.astype(BF16)
                to, copy = yb_copy(k, j)
                pl.when(to != x)(copy.start)

        return carry

    def turned_weights(it, carry):
        sp, hp, rows, lanes, half, half_lanes = where_of(it)
        for u in (0, 1):
            i = sp * 16 + 2 * hp + u
            col = S.la[2 * hp + u, rows, :]
            line = S.la_row[i, 0:1, :]
            tl = jnp.exp(jnp.where(upper, line[:, :128] - col[:128], NEG))
            tr = jnp.exp(line[:, 128:] - col[:128])
            br = jnp.exp(jnp.where(upper, line[:, 128:] - col[128:], NEG))
            S.within_t[i, 0] = tl.astype(BF16)
            S.within_t[i, 1] = tr.astype(BF16)
            S.within_t[i, 2] = br.astype(BF16)
            S.weights_t[i, 0] = (tl * S.aff_t[sp, :128, :128]).astype(BF16)
            S.weights_t[i, 1] = (tr * S.aff_t[sp, :128, 128:]).astype(BF16)
            S.weights_t[i, 2] = (br * S.aff_t[sp, 128:, 128:]).astype(BF16)
        return carry

    scan_copy.wait_recv()

    def ring_pair(i, carry):
        pl.when(i > 0)(lambda: ring_step(2 * i + 1))
        lax.fori_loop(jnp.where(i == 0, 0, 2 * i + 1), 2 * i + 3, weight_part, 0)
        lax.fori_loop(6 * i, jnp.minimum(6 * i + 6, 16), turned_weights, 0)
        lax.fori_loop(1, jnp.where(i == 2, 3, 1), weight_turn, 0)
        ring_step(2 * i + 2)
        lax.fori_loop(0, jnp.where(i == 1, 1, 0), weight_turn, 0)
        return carry

    lax.fori_loop(0, 3, ring_pair, 0)

    def pull(it, carry):
        sp, hp, rows, lanes, half, half_lanes = where_of(it)
        grad = S.y_acc[rows, lanes].astype(BF16)
        S.gy[rows, lanes] = grad
        scaled = (jnp.exp(pair_log(rows, hp)) * grad.astype(F32)).astype(BF16)
        S.gy_start[rows, lanes] = scaled
        S.adds[sp, half, :, half_lanes] = mm(S.c_t[sp], scaled)
        return carry

    lax.fori_loop(0, 16, pull, 0, unroll=8)
    for half in (0, 1):
        S.loc[1, half] = S.adds[0, half] + jnp.exp(S.tots[0, half, 0:1, :]) * S.adds[1, half]
    exchange_1(1)
    weight_part(7, 0)
    exchange_2(1)
    lax.fori_loop(3, 5, weight_turn, 0)

    def within_back(it, carry):
        sp, hp, rows, lanes, half, half_lanes = where_of(it)
        values = S.xv[rows, lanes]
        grads = S.gy[rows, lanes]
        top = jnp.zeros((128, 128), F32)
        bottom = jnp.zeros((128, 128), F32)
        tl = jnp.zeros((128, 128), F32)
        tr = jnp.zeros((128, 128), F32)
        br = jnp.zeros((128, 128), F32)
        for u in (0, 1):
            i = sp * 16 + 2 * hp + u
            mine = values * lane_masks[u]
            grad = grads * lane_masks[u]
            pair_top = mm_nt(mine[:128], grads)
            pair_bottom = mm_nt(mine[128:], grads[128:])
            tl += pair_top[:, :128] * S.within_t[i, 0].astype(F32)
            tr += pair_top[:, 128:] * S.within_t[i, 1].astype(F32)
            br += pair_bottom * S.within_t[i, 2].astype(F32)
            top += mm(jnp.concatenate([S.weights_t[i, 0], S.weights_t[i, 1]], axis=1), grad)
            bottom += mm(S.weights_t[i, 2], grad[128:])
        S.inner[at256(sp, 128), lanes] = top
        S.inner[at128(2 * sp + 1), lanes] = bottom
        S.aff_grad[sp, :128, :128] += tl
        S.aff_grad[sp, :128, 128:] += tr
        S.aff_grad[sp, 128:, 128:] += br
        return carry

    S.aff_grad[...] = jnp.zeros_like(S.aff_grad)
    lax.fori_loop(0, 16, within_back, 0, unroll=8)

    for sp in (0, 1):
        rows = pl.ds(sp * 256, 256)
        grad = mm_nt(S.gy_start[rows, :512], S.ent[sp, 0]) + mm_nt(S.gy_start[rows, 512:], S.ent[sp, 1])
        tl = S.aff_grad[sp, :128, :128].T.astype(BF16)
        tr = S.aff_grad[sp, :128, 128:].T.astype(BF16)
        br = S.aff_grad[sp, 128:, 128:].T.astype(BF16)
        writes = S.bv[rows, :]
        S.c_out[pl.ds(sp * 256, 128), :] = (grad[:128] + mm(tl, writes[:128])).astype(BF16)
        S.c_out[pl.ds(sp * 256 + 128, 128), :] = (
            grad[128:] + mm(jnp.concatenate([tr, br], axis=1), writes)
        ).astype(BF16)
    store_c = pltpu.make_async_copy(S.c_out, cg_hbm.at[0], S.store_sem.at[0])
    store_c.start()

    lax.fori_loop(5, 7, weight_turn, 0)
    exchange_3(1)
    weight_turn(7, 0)
    exchange_4(1)
    for half in (0, 1):
        S.lv[1, half] = S.inc[1, half].astype(BF16)
        S.lv[0, half] = (
            S.adds[1, half] + jnp.exp(S.tots[1, half, 0:1, :]) * S.inc[1, half]
        ).astype(BF16)

    def x_final(it, carry):
        sp, hp, rows, lanes, half, half_lanes = where_of(it)
        logs = pair_log(rows, hp)
        to_end = jnp.exp(logs[255:256, :] - logs)
        late = mm(S.bv[rows, :], S.lv[sp, half, :, half_lanes])
        S.x_out[rows, lanes] = (S.inner[rows, lanes] + to_end * late).astype(BF16)
        return carry

    lax.fori_loop(0, 16, x_final, 0, unroll=8)
    store_x = pltpu.make_async_copy(S.x_out, xg_hbm.at[0], S.store_sem.at[1])
    store_x.start()

    for sp in (0, 1):
        rows = pl.ds(sp * 256, 256)
        grad = mm_nt(S.x_end[rows, :512], S.lv[sp, 0]) + mm_nt(S.x_end[rows, 512:], S.lv[sp, 1])
        top = S.aff_grad[sp, :128, :].astype(BF16)
        br = S.aff_grad[sp, 128:, 128:].astype(BF16)
        reads = S.cv[rows, :]
        S.b_out[pl.ds(sp * 256, 128), :] = (grad[:128] + mm(top, reads)).astype(BF16)
        S.b_out[pl.ds(sp * 256 + 128, 128), :] = (grad[128:] + mm(br, reads[128:])).astype(BF16)
    store_b = pltpu.make_async_copy(S.b_out, bg_hbm.at[0], S.store_sem.at[2])
    store_b.start()

    for i in (0, 1, 2):
        wait_in(S.xb_in.at[i], S.xb_r_sem.at[i])
    total = S.xq[y].astype(F32)
    for i in (0, 1, 2):
        total = total + S.xb_in[i].astype(F32)
    S.w_out[pl.ds(0, X_ROWS), :] = total.astype(BF16)
    for i in (0, 1, 2):
        wait_in(S.yb_in.at[i], S.yb_r_sem.at[i])
    total = S.yq[x // 2, :, at128(x % 2)].astype(F32)
    for i in (0, 1, 2):
        total = total + S.yb_in[i].astype(F32)
    S.w_out[pl.ds(X_ROWS, Y_ROWS), :] = total.astype(BF16)
    store_w = pltpu.make_async_copy(S.w_out, wg_hbm, S.store_sem.at[3])
    store_w.start()

    def ring_sent(u, carry):
        for copy in ring(u, z, z):
            copy.wait_send()
        return carry

    lax.fori_loop(0, 7, ring_sent, 0)

    def block_sent(k, carry):
        for half in (0, 1):
            for copy in sib_columns(k, half):
                copy.wait_send()
        for j in (0, 1):
            to, copy = xa_copy(k, j)
            pl.when(to != x)(copy.wait_send)
        to, copy = ya_copy(k)
        pl.when(to != y)(copy.wait_send)

        @pl.when(x // 2 == k % 2)
        def _():
            to, copy = xb_copy(k)
            pl.when(to != y)(copy.wait_send)

        @pl.when(k // 2 == y)
        def _():
            for j in (0, 1):
                to, copy = yb_copy(k, j)
                pl.when(to != x)(copy.wait_send)

        return carry

    lax.fori_loop(0, 8, block_sent, 0)
    scan_copy.wait_send()
    d_sib_copy().wait_send()
    for dist in (1, 2, 3):
        d_chip_copy(dist).wait_send()
    for way in (0, 1):
        l1_copy(way).wait_send()
        l3_copy(way).wait_send()
        core, chip = place_of(way)
        for dist in (1, 2, 3):

            @pl.when(chip + dist <= 3)
            def _():
                l2_copy(way, dist).wait_send()

    for store in (store_c, store_x, store_b, store_w):
        store.wait()


def copy_kernel(*refs):
    ins, outs, held, sems = refs[:4], refs[4:8], refs[8:12], refs[12]
    pieces = []
    for n, size, count in ((1, 64, 8), (0, 256, 4), (2, 512, 1), (3, 512, 1)):
        src, dst, mid = ins[n], outs[n], held[n]
        for i in range(count):
            rows = pl.ds(i * size, size)
            at = (rows,) if n == 0 else (0, rows)
            j = 2 * len(pieces)
            pieces.append(
                (
                    pltpu.make_async_copy(src.at[at], mid.at[at], sems.at[j]),
                    pltpu.make_async_copy(mid.at[at], dst.at[at], sems.at[j + 1]),
                )
            )
    for come, _ in pieces:
        come.start()
    for come, go in pieces:
        come.wait()
        go.start()
    for _, go in pieces:
        go.wait()


def per_device(x_in, b_in, c_in, log_decay, out_weight, out_grad):
    out_shape = (
        jax.ShapeDtypeStruct((1024, 128), BF16),
        jax.ShapeDtypeStruct((1, 512, 1024), BF16),
        jax.ShapeDtypeStruct((1, 512, 128), BF16),
        jax.ShapeDtypeStruct((1, 512, 128), BF16),
    )
    scratch = [pltpu.VMEM(shape, dtype) for shape, dtype in VMEM_SCRATCH.values()]
    scratch += [pltpu.SemaphoreType.DMA(shape) for shape in SEMAPHORES.values()]
    results = pl.pallas_call(
        kernel,
        out_shape=out_shape,
        in_specs=[pl.BlockSpec(memory_space=pl.ANY)] * 6,
        out_specs=[pl.BlockSpec(memory_space=pl.ANY)] * 4,
        scratch_shapes=scratch,
        compiler_params=pltpu.CompilerParams(
            collective_id=0, has_side_effects=True, vmem_limit_bytes=63 * 2**20
        ),
    )(x_in, b_in, c_in, jnp.transpose(log_decay, (0, 2, 1)), out_weight, out_grad)
    return pl.pallas_call(
        copy_kernel,
        out_shape=out_shape,
        in_specs=[pl.BlockSpec(memory_space=pl.ANY)] * 4,
        out_specs=[pl.BlockSpec(memory_space=pl.ANY)] * 4,
        scratch_shapes=[pltpu.VMEM(o.shape, o.dtype) for o in out_shape]
        + [pltpu.SemaphoreType.DMA((28,))],
    )(*results)


def solution(mesh):
    in_specs = (
        P("dp", "seq", "tensor"),
        P("dp", "seq", "tensor"),
        P("dp", "seq", "tensor"),
        P("dp", "seq", "tensor"),
        P("tensor", None),
        P("dp", "seq", "tensor"),
    )
    out_specs = (
        P("tensor", ("dp", "seq")),
        P("dp", "seq", "tensor"),
        P("dp", "seq", "tensor"),
        P("dp", "seq", "tensor"),
    )
    return jax.shard_map(
        per_device, mesh=mesh, in_specs=in_specs, out_specs=out_specs, check_vma=False
    )
```
